512 devices in a mesh: sec: 128 (over x_lo, z, y), tp: 4 (over x_hi, core).
Axes of the slice: x: 4 (x_hi: 2, x_lo: 2; x = x_hi * 2 + x_lo), y: 8, z: 8, core: 2. Of those that a mesh axis runs over, the one named last changes fastest.
Arguments:
- store: bfloat16 [128, 4, 2359296], P('sec', 'tp'), may hold values from -9 to 9
- queries: bfloat16 [256, 128, 576], P('sec'), may hold values from -54 to 54
- new_latent: bfloat16 [256, 576], P('sec'), may hold values from -6 to 6
- cached_len: int32 [256], P('sec'), may hold values from 512 to 2048
- rows: bfloat16 [2048, 7168], P('sec', 'tp'), may hold values from -6 to 6
- expert_ids: int32 [2048, 8], P('sec'), may hold values from 0 to 255, all different within a row; in each aligned block of 16 rows (0 to 15, 16 to 31, ...) at most 5 rows name the same one
- route_gates: float32 [2048, 8], P('sec'), may hold values from 0.05 to 0.6
- capacity: int32 [128, 32], P('sec'), may hold values from 2 to 3
Outputs:
- attended: bfloat16 [256, 128, 512], P('sec', 'tp')
- mixed: bfloat16 [2048, 7168], P('sec', 'tp')
The draws below stay inside these ranges and needn't reach their ends.
Inputs may be any that keep to these rules, and one draw needn't show every extreme that they name: `expert_ids`: each row names 8 different experts; at most 5 of the rows of one sec index name the same expert.
All inputs are finite; a program needn't handle non-finite values.
Results may differ from the reference program's by a relative error of at most 0.017.
Values may be sent and summed in bfloat16 or wider, within the bound.
No kernel may reach another device: no remote copies, remote signals or barrier semaphores. Data moves between devices by JAX's collectives and lax.ppermute only.
A program may use at most 128 MiB of HBM per device.

```python
import math
import jax
import jax.numpy as jnp
import numpy as np
from jax import lax

D = 7168
H = 128
LATENT = 512
E_ALL = 256
TOP = 8
FF_WIN = 1152
LEN = 2048
RQ = 2
RB = 16
KV = 576
LP = 512
HD = 96
CAP = 3
STORE = 2359296
N_SEC = 128
N_TP = 4


def latent_keys(key):
    return jnp.clip(jax.random.normal(jax.random.fold_in(key, 11), (N_SEC // 4, 4 * RQ, KV), jnp.float32), -6.0, 6.0)


def draw_store(key, part):
    anchors = latent_keys(key)
    key = jax.random.fold_in(key, 1)
    servers = N_SEC // 4
    cache = jnp.clip(jax.random.normal(jax.random.fold_in(key, 2), (servers, N_TP, 4 * RQ, LP, KV), jnp.float32), -6.0, 6.0)
    cache = cache.at[:, 0, :, 0, :].set(anchors)
    cache_el = 4 * RQ * LP * KV
    cache = cache.reshape(servers, N_TP, cache_el)
    cache = jnp.pad(cache, ((0, 0), (0, 0), (0, STORE - cache_el))).astype(jnp.bfloat16)
    span_w = D * HD
    paired = jnp.clip(jax.random.normal(jax.random.fold_in(key, 4), (N_SEC - servers, N_TP, 2 * span_w), jnp.float32), -6.0, 6.0) * D ** (-0.5)
    lowered = jnp.clip(jax.random.normal(jax.random.fold_in(key, 5), (N_SEC - servers, N_TP, span_w), jnp.float32), -6.0, 6.0) * FF_WIN ** (-0.5)
    weights = jnp.concatenate([paired, lowered], axis=2)
    weights = jnp.pad(weights, ((0, 0), (0, 0), (0, STORE - 3 * span_w))).astype(jnp.bfloat16)
    return jnp.concatenate([cache, weights], axis=0)


def draw_queries(key, part):
    key = jax.random.fold_in(key, 7)
    values = jnp.clip(jax.random.normal(key, (N_SEC * RQ, H, KV), jnp.float32), -6.0, 6.0)
    return values.astype(jnp.bfloat16)


def draw_cached_len(key, part):
    key = jax.random.fold_in(key, 13)
    count = N_SEC * RQ
    lengths = jax.random.randint(jax.random.fold_in(key, 1), (count,), LEN // 4, LEN + 1, jnp.int32)
    first = jax.random.randint(jax.random.fold_in(key, 2), (), 0, count, jnp.int32)
    lengths = lengths.at[first].set(LEN)
    lengths = lengths.at[(first + 1) % count].set(LEN // 4)
    return lengths


def draw_capacity(key, part):
    key = jax.random.fold_in(key, 17)
    count = N_SEC * (N_SEC // 4)
    limits = jax.random.randint(jax.random.fold_in(key, 1), (count,), 2, CAP + 1, jnp.int32)
    first = jax.random.randint(jax.random.fold_in(key, 2), (), 0, count, jnp.int32)
    limits = limits.at[first].set(CAP)
    limits = limits.at[(first + 1) % count].set(2)
    return limits.reshape(N_SEC, N_SEC // 4)


def shard_levels(rng, shape, split, least, top_value):
    gain, own = 1.0, jax.random.fold_in(rng, 6)
    for axis_at, parts in split:
        steps = jnp.exp(jax.random.uniform(jax.random.fold_in(own, axis_at), (parts,), jnp.float32, least / len(split), top_value / len(split)))
        gain = gain * jnp.repeat(steps, shape[axis_at] // parts).reshape([-1 if axis == axis_at else 1 for axis in range(len(shape))])
    return gain


def deal_out(rng, own, number, rows, count, top, bound, slope):
    sequence = jax.random.permutation(rng, count)
    packed, usual = portions_of(count, rows * top, bound, slope, True), portions_of(count, rows * top, bound, slope, False)
    places = jnp.arange(count)

    def named(tallies, offset_by):
        used = int((tallies > 0).sum())
        fixed = max(1, used // 4)
        moved = fixed + (places - fixed + offset_by * (used - fixed)) % max(1, count - fixed)
        return jnp.zeros((count,), jnp.int32).at[sequence[jnp.where(places < fixed, places, moved)]].set(jnp.asarray(tallies, jnp.int32))

    tallies = jnp.where(number % 4 == 0, named(packed, number // 4), named(usual, number - number // 4 - 1))
    mixed = jax.random.permutation(jax.random.fold_in(own, 3), count)
    source_of, receiver = mixed[0:count // 2 * 2:2], mixed[1:count // 2 * 2:2]
    slack = jnp.minimum(tallies[source_of] - 1, bound - tallies[receiver]) // 2
    slack = jnp.where((source_of == sequence[0]) | (receiver == sequence[0]) | (tallies[receiver] == 0), 0, jnp.maximum(slack, 0))
    moved = jax.random.randint(jax.random.fold_in(own, 4), (count // 2,), 0, 1 << 20) % (slack + 1)
    tallies = tallies.at[source_of].add(-moved).at[receiver].add(moved)
    items = jnp.searchsorted(jnp.cumsum(tallies), jnp.arange(rows * top), side="right").astype(jnp.int32)
    table = items.reshape(top, rows).T
    table = table[jax.random.permutation(jax.random.fold_in(own, 1), rows)]
    offset_by = jax.random.randint(jax.random.fold_in(own, 2), (rows, 1), 0, top)
    return jnp.take_along_axis(table, (jnp.arange(top)[None, :] + offset_by) % top, axis=1)


def portions_of(amount, total, reach, lean, full):
    portions = [(1 << 20) // math.isqrt(standing ** lean) + 1 for standing in range(1, amount + 1)]
    largest = reach if full else min(reach, max(-(-total // amount), total * portions[0] // sum(portions)))
    least = 1 if total - largest >= amount - 1 else 0
    given, rest = [largest] + [least] * (amount - 1), total - largest - least * (amount - 1)
    while rest > 0:
        movable = [i for i in range(1, amount) if given[i] < largest] or [i for i in range(1, amount) if given[i] < reach]
        pool, remaining = sum([portions[i] for i in movable]), rest
        for i in movable:
            addition = min(reach - given[i], max(1, remaining * portions[i] // pool), rest)
            given[i] = given[i] + addition
            rest = rest - addition
    return np.array(given)


def centred(own_key, dims, width, bound, shards=(), held_as=jnp.bfloat16):
    values = jax.random.normal(own_key, dims, jnp.float32) * width
    if len(shards) > 0:
        values = shard_levels(own_key, dims, shards, -0.22, 0.18) * values
    return jnp.clip(values, min=-bound, max=bound).astype(held_as)


def setup_inputs(seed: int = 0) -> dict:
    key_list = jax.random.split(jax.random.key(seed), 9)
    store = draw_store(jax.random.fold_in(key_list[8], 71), 0)
    queries = draw_queries(jax.random.fold_in(key_list[8], 71), 0)
    new_latent = centred(key_list[2], (N_SEC * RQ, KV), 1.5, 6.0, ((0, 128),))
    cached_len = draw_cached_len(jax.random.fold_in(key_list[8], 71), 0)
    rows = centred(key_list[4], (N_SEC * RB, D), 1.0, 6.0, ((0, 128), (1, 4)))
    expert_ids_keys = jax.random.split(jax.random.fold_in(key_list[5], 1), (N_SEC * RB) // RB)
    expert_ids_turns = jax.random.permutation(jax.random.fold_in(key_list[5], 3), (N_SEC * RB) // RB)
    expert_ids = jax.vmap(lambda own, number: deal_out(jax.random.fold_in(key_list[5], 2), own, number, RB, E_ALL, TOP, CAP + 2, 2))(expert_ids_keys, expert_ids_turns).reshape((N_SEC * RB, TOP))
    route_gates = jnp.clip(0.05 + 0.55 * jax.random.uniform(key_list[6], (N_SEC * RB, TOP), jnp.float32) ** shard_levels(key_list[6], (N_SEC * RB, TOP), ((0, 128),), -0.2, 0.2), 0.05, 0.6)
    capacity = draw_capacity(jax.random.fold_in(key_list[8], 71), 0)
    return {"store": store, "queries": queries, "new_latent": new_latent, "cached_len": cached_len, "rows": rows, "expert_ids": expert_ids, "route_gates": route_gates, "capacity": capacity}


softmax_scale = 1.0 / math.sqrt(192.0)

def reference(store, queries, new_latent, cached_len, rows, expert_ids, route_gates, capacity):
    servers = N_SEC // 4
    cache_el = 4 * RQ * LP * KV
    cache = store[:servers, :, :cache_el].reshape(servers, N_TP, 4, RQ, LP, KV)
    cache = jnp.transpose(cache, (2, 0, 3, 1, 4, 5)).reshape(N_SEC * RQ, LEN, KV)

    def attend(item):
        query, keys, fresh, length = item
        query_f = query.astype(jnp.float32)
        keys_f = keys.astype(jnp.float32)
        fresh_f = fresh.astype(jnp.float32)
        scores = jnp.dot(query_f, keys_f.T) * softmax_scale
        own = jnp.dot(query_f, fresh_f) * softmax_scale
        live = jnp.arange(LEN, dtype=jnp.int32) < length
        masked = jnp.where(live[None, :], scores, -1e+30)
        top = jnp.maximum(lax.optimization_barrier(jnp.max(masked, axis=1)), own)
        weights = jnp.where(live[None, :], jnp.exp(masked - top[:, None]), 0.0).astype(jnp.bfloat16)
        weights = lax.optimization_barrier(weights).astype(jnp.float32)
        own_weight = jnp.exp(own - top).astype(jnp.bfloat16)
        own_weight = lax.optimization_barrier(own_weight).astype(jnp.float32)
        total = lax.optimization_barrier(jnp.sum(weights, axis=1)) + own_weight
        summed = jnp.dot(weights, keys_f[:, :LATENT]) + own_weight[:, None] * fresh_f[None, :LATENT]
        return (summed / total[:, None]).astype(jnp.bfloat16)
    attended = lax.map(attend, (queries, cache, new_latent, cached_len))
    experts = N_SEC // 4
    labels = jnp.arange(experts, dtype=jnp.int32)
    match = expert_ids[:, :, None] == labels[None, None, :]
    hits = jnp.any(match, axis=1).astype(jnp.int32).reshape(N_SEC, RB, experts)
    gate_of = lax.optimization_barrier(jnp.sum(jnp.where(match, route_gates[:, :, None], 0.0), axis=1)).reshape(N_SEC, RB, experts)
    rank = jnp.cumsum(hits, axis=1) - hits
    keep = (hits == 1) & (rank < capacity[:, None, :])
    slots = jnp.arange(CAP, dtype=jnp.int32)
    place = keep[:, :, :, None] & (rank[:, :, :, None] == slots[None, None, None, :])
    blocks = rows.reshape(N_SEC, RB, D).astype(jnp.float32)
    span_w = D * HD

    def expert_out(carry, index):
        pick = place[:, :, index, :].astype(jnp.float32)
        chosen = jnp.einsum('src,srd->scd', pick, blocks).astype(jnp.bfloat16).reshape(N_SEC * CAP, D)
        held = lax.dynamic_slice_in_dim(store, (servers + 3 * index).astype(jnp.int32), 3, 0)
        gate_w = held[:, :, :span_w].reshape(3, N_TP, D, HD).transpose(2, 0, 1, 3).reshape(D, FF_WIN)
        up_w = held[:, :, span_w:2 * span_w].reshape(3, N_TP, D, HD).transpose(2, 0, 1, 3).reshape(D, FF_WIN)
        down_w = held[:, :, 2 * span_w:3 * span_w].reshape(3, N_TP, N_TP * HD, D // N_TP)
        gate = jnp.dot(chosen, gate_w, preferred_element_type=jnp.float32)
        upper = jnp.dot(chosen, up_w, preferred_element_type=jnp.float32)
        hidden = (jax.nn.silu(gate) * upper).astype(jnp.bfloat16).reshape(N_SEC * CAP, 3, N_TP * HD)
        result = jnp.zeros((N_SEC * CAP, D), jnp.float32)
        for third in range(3):
            down_j = down_w[third].transpose(1, 0, 2).reshape(N_TP * HD, D)
            piece = jnp.dot(hidden[:, third], down_j, preferred_element_type=jnp.float32).astype(jnp.bfloat16)
            result = result + lax.optimization_barrier(piece).astype(jnp.float32)
        result = result.reshape(N_SEC, CAP, D)
        scaled = pick * gate_of[:, :, index][:, :, None]
        return (carry + jnp.einsum('src,scd->srd', scaled, result), None)
    total, _ = lax.scan(expert_out, jnp.zeros((N_SEC, RB, D), jnp.float32), labels)
    mixed = total.reshape(N_SEC * RB, D).astype(jnp.bfloat16)
    return (attended, mixed)
```

```python
import functools
import math

import jax
import jax.numpy as jnp
from jax import lax
from jax.experimental import pallas as pl
from jax.experimental.pallas import tpu as pltpu
from jax.sharding import PartitionSpec as P

LATENT = 512
KV = 576
LP = 512
CAP = 3
HD = 96
DQ = 1792
PART = 640
f32 = jnp.float32
bf16 = jnp.bfloat16
VM = 48 << 20

softmax_scale = 1.0 / math.sqrt(192.0)


def dot(a, b, dims=((1,), (0,))):
    return lax.dot_general(a, b, (dims, ((), ())), preferred_element_type=f32)


def pieces(value):
    high = value.astype(bf16).astype(f32)
    middle = (value - high).astype(bf16).astype(f32)
    return high, middle, value - high - middle


def flat_rows(s_ref, scr):
    scr[...] = s_ref[...].astype(f32).reshape(scr.shape)


def dispatch_kernel(sel_ref, rows_ref, out_ref):
    source = lax.broadcasted_iota(jnp.int32, (256, 256), 0)
    target = lax.broadcasted_iota(jnp.int32, (256, 256), 1)
    order = (source == 4 * (target % 64) + target // 64).astype(f32).astype(bf16)
    for b in range(DQ // 256):
        span = slice(256 * b, 256 * b + 256)
        turned = dot(rows_ref[:, span], order).astype(bf16)
        for c in range(CAP):
            out_ref[:, DQ * c + 256 * b : DQ * c + 256 * b + 256] = dot(sel_ref[c], turned).astype(bf16)


def attend_kernel(info_ref, s_ref, q_ref, p_ref, scr, keys):
    row = pl.program_id(0)
    flat_rows(s_ref, scr)
    for m in range(9):
        keys[:, 128 * m : 128 * m + 128] = scr[pl.ds(m, LP // 2, stride=9), :].astype(bf16)
    lane = lax.broadcasted_iota(jnp.int32, (128, PART), 1)
    even_q = jnp.where(lane < KV, q_ref[0].astype(f32), 0.0)
    odd_q = pltpu.roll(even_q, 64, 1).astype(bf16)
    even_q = even_q.astype(bf16)
    even = dot(even_q, keys[:, :640], ((1,), (1,))) * softmax_scale
    odd = dot(odd_q, keys[:, 512:], ((1,), (1,))) * softmax_scale
    left = info_ref[row] - info_ref[8]
    position = 2 * lax.broadcasted_iota(jnp.int32, (128, LP // 2), 1)
    even = jnp.where(position < left, even, -1e30)
    odd = jnp.where(position + 1 < left, odd, -1e30)
    top = jnp.maximum(jnp.max(even, axis=1, keepdims=True), jnp.max(odd, axis=1, keepdims=True))
    even = jnp.where(position < left, jnp.exp(even - top), 0.0).astype(bf16)
    odd = jnp.where(position + 1 < left, jnp.exp(odd - top), 0.0).astype(bf16)
    total = jnp.sum(even.astype(f32), axis=1, keepdims=True) + jnp.sum(odd.astype(f32), axis=1, keepdims=True)
    summed = dot(even, keys[:, :LATENT]) + dot(odd, keys[:, 512:])[:, 64 : 64 + LATENT]
    summed = summed.astype(bf16)
    lane = lax.broadcasted_iota(jnp.int32, (128, 128), 1)
    stats = jnp.zeros((128, 128), f32)
    for at, piece in enumerate(pieces(top) + pieces(total)):
        stats = jnp.where(lane == at, piece, stats)
    stats = stats.astype(bf16)
    first = pl.ds(pl.multiple_of(row * 32, 32), 32)
    second = pl.ds(pl.multiple_of(256 + row * 32, 32), 32)
    for t in range(4):
        heads = slice(32 * t, 32 * t + 32)
        p_ref[t, first, :] = summed[heads, :384]
        p_ref[t, second, 0:128] = summed[heads, 384:]
        p_ref[t, second, 128:256] = stats[heads]


def attend(store, asked, info):
    return pl.pallas_call(
        attend_kernel,
        grid_spec=pltpu.PrefetchScalarGridSpec(
            num_scalar_prefetch=1,
            grid=(8,),
            in_specs=[
                pl.BlockSpec((1, 1, LP * KV), lambda i, info: (0, 0, i)),
                pl.BlockSpec((1, 128, PART), lambda i, info: (i, 0, 0)),
            ],
            out_specs=pl.BlockSpec((4, 896, 384), lambda i, info: (0, 0, 0)),
            scratch_shapes=[pltpu.VMEM((LP * KV // 128, 128), f32), pltpu.VMEM((LP // 2, 2 * KV), bf16)],
        ),
        out_shape=jax.ShapeDtypeStruct((4, 896, 384), bf16),
        compiler_params=pltpu.CompilerParams(vmem_limit_bytes=VM),
    )(info, store, asked)


def unpack_kernel(s_ref, p_ref, w_ref, scr):
    step = pl.program_id(0)
    flat_rows(s_ref, scr)

    @pl.when(step < 8)
    def _():
        for m in range(3):
            p_ref[0, :, 128 * m : 128 * m + 128] = scr[pl.ds(m, 448, stride=3), :].astype(bf16)

    @pl.when(step >= 8)
    def _():
        for m in range(14):
            at = 128 * (m % 5)
            w_ref[m // 5, :, at : at + 128] = scr[pl.ds(m, HD, stride=14), :].astype(bf16)
        w_ref[2, :, 512:640] = jnp.zeros((HD, 128), bf16)


def unpack(store):
    return pl.pallas_call(
        unpack_kernel,
        grid=(12,),
        in_specs=[pl.BlockSpec((1, 1, DQ * HD), lambda i: (0, 0, i))],
        out_specs=[
            pl.BlockSpec((1, 448, 384), lambda i: (jnp.where(i < 8, i % 4, 3), jnp.where(i < 4, 0, 1), 0)),
            pl.BlockSpec((3, HD, PART), lambda i: (0, jnp.maximum(i - 8, 0), 0)),
        ],
        out_shape=[jax.ShapeDtypeStruct((4, 896, 384), bf16), jax.ShapeDtypeStruct((3, 384, PART), bf16)],
        scratch_shapes=[pltpu.VMEM((DQ * HD // 128, 128), f32)],
        compiler_params=pltpu.CompilerParams(vmem_limit_bytes=VM),
    )(store)


def weights_kernel(p_ref, w_ref):
    for half in range(2):
        for r in range(4):
            span = slice(HD * r, HD * r + HD)
            rows = slice(448 * half, 448 * half + 448)
            found = jnp.concatenate([p_ref[t, rows, span] for t in range(4)], axis=1)
            for b in range(7):
                w_ref[half, 256 * b + 64 * r : 256 * b + 64 * r + 64, :] = found[64 * b : 64 * b + 64]


def arrange(arrived):
    return pl.pallas_call(
        weights_kernel,
        out_shape=jax.ShapeDtypeStruct((2, DQ, 384), bf16),
        compiler_params=pltpu.CompilerParams(vmem_limit_bytes=VM),
    )(arrived)


def join_kernel(p_ref, out_ref):
    tops, totals = [], []
    for t in range(4):
        stats = p_ref[t, 256:512, 128:256].astype(f32)
        tops.append(stats[:, 0:1] + stats[:, 1:2] + stats[:, 2:3])
        totals.append(stats[:, 3:4] + stats[:, 4:5] + stats[:, 5:6])
    top = functools.reduce(jnp.maximum, tops)
    scales = [jnp.exp(own - top) for own in tops]
    total = sum(scale * own for scale, own in zip(scales, totals))
    scales = [scale / total for scale in scales]
    out_ref[:, :384] = sum(scales[t] * p_ref[t, 0:256, :].astype(f32) for t in range(4)).astype(bf16)
    out_ref[:, 384:512] = sum(scales[t] * p_ref[t, 256:512, 0:128].astype(f32) for t in range(4)).astype(bf16)
    lane = lax.broadcasted_iota(jnp.int32, (256, 128), 1)
    stats = jnp.zeros((256, 128), f32)
    for at, piece in enumerate(pieces(top + jnp.log(total))):
        stats = jnp.where(lane == at, piece, stats)
    out_ref[:, 512:640] = stats.astype(bf16)


def join(arrived):
    return pl.pallas_call(
        join_kernel,
        out_shape=jax.ShapeDtypeStruct((256, PART), bf16),
        compiler_params=pltpu.CompilerParams(vmem_limit_bytes=VM),
    )(arrived)


def project_kernel(x_ref, w_ref, z_ref):
    for half in range(2):
        turned = dot(x_ref[...], w_ref[half]).T.astype(bf16)
        for t in range(4):
            z_ref[t, HD * half : HD * half + HD, :] = turned[HD * t : HD * t + HD]


def project(slab, weights):
    return pl.pallas_call(
        project_kernel,
        grid=(CAP,),
        in_specs=[
            pl.BlockSpec((128, DQ), lambda c: (0, c)),
            pl.BlockSpec((2, DQ, 384), lambda c: (0, 0, 0)),
        ],
        out_specs=pl.BlockSpec((4, 2 * HD, 128), lambda c: (0, 0, c)),
        out_shape=jax.ShapeDtypeStruct((4, 2 * HD, 384), bf16),
        compiler_params=pltpu.CompilerParams(vmem_limit_bytes=VM),
    )(slab, weights)


def descend_kernel(h_ref, w0_ref, w1_ref, w2_ref, out_ref, scr):
    result = jnp.zeros((384, PART), f32)
    for d, w_ref in enumerate((w0_ref, w1_ref, w2_ref)):
        for t in range(4):
            scr[HD * t : HD * t + HD, :] = h_ref[t, d]
        result = result + dot(scr[...], w_ref[...], ((0,), (0,)))
    for c in range(CAP):
        out_ref[:, PART * c : PART * c + PART] = result[128 * c : 128 * c + 128].astype(bf16)


def descend(hidden, w0, w1, w2):
    return pl.pallas_call(
        descend_kernel,
        out_shape=jax.ShapeDtypeStruct((128, CAP * PART), bf16),
        scratch_shapes=[pltpu.VMEM((384, 384), bf16)],
        compiler_params=pltpu.CompilerParams(vmem_limit_bytes=VM),
    )(hidden, w0, w1, w2)


def combine_kernel(a_ref, x_ref, out_ref):
    result = jnp.zeros((48, PART), f32)
    for c in range(CAP):
        block = x_ref[:, PART * c : PART * c + PART]
        both = dot(a_ref[c], block)
        result = result + (both[:48] + both[48:])
    result = result.astype(bf16)
    out_ref[:, 0:640] = result[0:16]
    out_ref[:, 640:1280] = result[16:32]
    out_ref[:, 1280:1792] = result[32:48, :512]


def per_device(store, queries, new_latent, cached_len, rows, expert_ids, route_gates, capacity):
    groups = lax.axis_size("sec")
    servers = groups // 4
    place = lax.axis_index("sec")
    part = lax.axis_index("tp")
    serving = place < servers
    both = ("sec", "tp")
    core = part % 2

    experts = capacity.shape[1]
    labels = jnp.arange(experts, dtype=jnp.int32)
    match = expert_ids[:, :, None] == labels[None, None, :]
    hits = jnp.any(match, axis=1).astype(jnp.int32)
    gate_of = jnp.sum(jnp.where(match, route_gates[:, :, None], 0.0), axis=1)
    rank = jnp.cumsum(hits, axis=0) - hits
    keep = (hits == 1) & (rank < capacity[0][None, :])
    slots = jnp.arange(CAP, dtype=jnp.int32)
    pick = (keep[None] & (rank[None] == slots[:, None, None])).astype(f32)
    spread = jnp.pad(jnp.repeat(pick, 3, axis=2), ((0, 0), (0, 0), (servers, 0)))
    sel = jnp.swapaxes(spread, 1, 2).astype(bf16)
    outgoing = pl.pallas_call(
        dispatch_kernel, out_shape=jax.ShapeDtypeStruct((groups, CAP * DQ), bf16)
    )(sel, rows)
    arrived = lax.all_to_all(outgoing, "sec", split_axis=0, concat_axis=0, tiled=True)

    digits = jnp.stack([cached_len // 64, cached_len % 64], axis=1).astype(bf16)
    digits = jnp.pad(digits, ((0, 0), (0, PART - KV - 2)))
    asked = jnp.concatenate([queries, jnp.broadcast_to(digits[:, None, :], (2, 128, PART - KV))], axis=2)
    half = lax.dynamic_slice_in_dim(asked, core * 64, 64, 1)
    incoming = [half]
    for k in range(1, 4):
        incoming.append(lax.ppermute(half, "sec", [(k * servers + a, a) for a in range(servers)]))
    half = jnp.concatenate(incoming, axis=0)
    other = lax.ppermute(half, both, [(4 * a + t, 4 * a + (t ^ 1)) for a in range(servers) for t in range(4)])
    asked = jnp.concatenate([jnp.where(core == 0, half, other), jnp.where(core == 0, other, half)], axis=1)
    lengths = asked[:, 0, KV].astype(jnp.int32) * 64 + asked[:, 0, KV + 1].astype(jnp.int32)
    info = jnp.concatenate([lengths, (part * LP).reshape(1).astype(jnp.int32)])

    def serve():
        return attend(store, asked, info), jnp.zeros((3, 384, PART), bf16)

    payload, down = lax.cond(serving, serve, lambda: tuple(unpack(store)))
    arranged = lax.all_to_all(payload, "tp", split_axis=0, concat_axis=0, tiled=True)

    def sibling(value, step):
        return lax.ppermute(
            value,
            "sec",
            [(servers + 3 * e + j, servers + 3 * e + (j + step) % 3) for e in range(experts) for j in range(3)],
        )

    third = (place - servers) % 3
    downs = [lax.dynamic_index_in_dim(down, third, 0, keepdims=False)]
    for step in (1, 2):
        downs.append(sibling(lax.dynamic_index_in_dim(down, (third + step) % 3, 0, keepdims=False), step))

    answer, weights = lax.cond(
        serving,
        lambda: (join(arranged), jnp.zeros((2, DQ, 384), bf16)),
        lambda: (jnp.zeros((256, PART), bf16), arrange(arranged)),
    )

    answer = answer.reshape(4, 64, PART)
    returned = answer[0]
    for k in range(1, 4):
        returned = returned + lax.ppermute(answer[k], "sec", [(a, k * servers + a) for a in range(servers)])
    mine = lax.dynamic_slice_in_dim(queries, part * 32, 32, 1)
    own = jnp.einsum("rhk,rk->rh", mine, new_latent, preferred_element_type=f32) * softmax_scale
    own = own[:, :, None]
    returned = returned.reshape(2, 32, PART).astype(f32)
    others = returned[:, :, 512:513] + returned[:, :, 513:514] + returned[:, :, 514:515]
    top = jnp.maximum(own, others)
    own, others = jnp.exp(own - top), jnp.exp(others - top)
    attended = (others * returned[:, :, :LATENT] + own * new_latent[:, None, :LATENT].astype(f32)) / (own + others)
    attended = attended.astype(bf16)

    partial = lax.cond(
        serving, lambda: jnp.zeros((4, 2 * HD, 384), bf16), lambda: project(arrived, weights)
    )
    partial = lax.all_to_all(partial, "tp", split_axis=0, concat_axis=0, tiled=True)
    partial = jnp.sum(partial.astype(f32), axis=0)
    hidden = (jax.nn.silu(partial[:HD]) * partial[HD:]).astype(bf16)
    hidden = jnp.stack([hidden, sibling(hidden, 1), sibling(hidden, 2)])
    hidden = lax.all_gather(hidden, "tp", axis=0)
    result = lax.cond(
        serving, lambda: jnp.zeros((groups, CAP * PART), bf16), lambda: descend(hidden, *downs)
    )
    result = lax.all_to_all(result, "sec", split_axis=0, concat_axis=0, tiled=True)

    scaled = spread * jnp.pad(jnp.repeat(gate_of, 3, axis=1), ((0, 0), (servers, 0)))[None]
    holder = (jnp.arange(groups) - servers) % 3
    scaled = jnp.where(holder == jnp.arange(3)[:, None, None, None], scaled[None], 0.0)
    scaled = jnp.swapaxes(scaled, 0, 1).reshape(CAP, 48, groups)
    high = lax.reduce_precision(scaled, 8, 7)
    weight = jnp.concatenate([high, scaled - high], axis=1).astype(bf16)
    mixed = pl.pallas_call(
        combine_kernel, out_shape=jax.ShapeDtypeStruct((16, DQ), bf16)
    )(weight, result)
    return (attended, mixed)


def solution(mesh):
    placed = (
        P("sec", "tp", None),
        P("sec", None, None),
        P("sec", None),
        P("sec"),
        P("sec", "tp"),
        P("sec", None),
        P("sec", None),
        P("sec", None),
    )
    return jax.shard_map(
        per_device,
        mesh=mesh,
        in_specs=placed,
        out_specs=(P("sec", "tp", None), P("sec", "tp")),
        check_vma=False,
    )
```

```python
import functools
import math

import jax
import jax.numpy as jnp
from jax import lax
from jax.experimental import pallas as pl
from jax.experimental.pallas import tpu as pltpu
from jax.sharding import PartitionSpec as P

LATENT = 512
KV = 576
LP = 512
CAP = 3
HD = 96
DQ = 1792
PART = 640
f32 = jnp.float32
bf16 = jnp.bfloat16
VM = 48 << 20

softmax_scale = 1.0 / math.sqrt(192.0)


def dot(a, b, dims=((1,), (0,))):
    return lax.dot_general(a, b, (dims, ((), ())), preferred_element_type=f32)


def pieces(value):
    high = value.astype(bf16).astype(f32)
    middle = (value - high).astype(bf16).astype(f32)
    return high, middle, value - high - middle


def flat_rows(s_ref, scr):
    scr[...] = s_ref[...].astype(f32).reshape(scr.shape)


def dispatch_kernel(sel_ref, rows_ref, out_ref, scr):
    source = lax.broadcasted_iota(jnp.int32, (256, 256), 0)
    target = lax.broadcasted_iota(jnp.int32, (256, 256), 1)
    order = (source == 4 * (target % 64) + target // 64).astype(f32).astype(bf16)
    count = out_ref.shape[0]
    for b in range(DQ // 256):
        turned = dot(rows_ref[:, 256 * b : 256 * b + 256], order).astype(bf16)
        for c in range(CAP):
            sent = dot(sel_ref[c], turned)
            for k in range(2):
                scr[pl.ds(16 * c + 2 * b + k, count, stride=48), :] = sent[:, 128 * k : 128 * k + 128]
    for c in range(CAP):
        for k in range(14, 16):
            scr[pl.ds(16 * c + k, count, stride=48), :] = jnp.zeros((count, 128), f32)
    out_ref[...] = scr[...].astype(bf16).reshape(out_ref.shape)


def dispatch(sel, rows):
    groups = sel.shape[1]
    return pl.pallas_call(
        dispatch_kernel,
        out_shape=jax.ShapeDtypeStruct((groups, 48, 128), bf16),
        scratch_shapes=[pltpu.VMEM((groups * 48, 128), f32)],
        compiler_params=pltpu.CompilerParams(vmem_limit_bytes=VM),
    )(sel, rows)


def attend_kernel(info_ref, s_ref, q_ref, *refs):
    p_refs, (scr, keys, found) = refs[:4], refs[4:]
    row = pl.program_id(0)
    flat_rows(s_ref, scr)
    for m in range(9):
        keys[:, 128 * m : 128 * m + 128] = scr[pl.ds(m, LP // 2, stride=9), :].astype(bf16)
    lane = lax.broadcasted_iota(jnp.int32, (128, PART), 1)
    even_q = jnp.where(lane < KV, q_ref[0].astype(f32), 0.0)
    odd_q = pltpu.roll(even_q, 64, 1).astype(bf16)
    even_q = even_q.astype(bf16)
    even = dot(even_q, keys[:, :640], ((1,), (1,))) * softmax_scale
    odd = dot(odd_q, keys[:, 512:], ((1,), (1,))) * softmax_scale
    left = info_ref[row] - info_ref[8]
    position = 2 * lax.broadcasted_iota(jnp.int32, (128, LP // 2), 1)
    even = jnp.where(position < left, even, -1e30)
    odd = jnp.where(position + 1 < left, odd, -1e30)
    top = jnp.maximum(jnp.max(even, axis=1, keepdims=True), jnp.max(odd, axis=1, keepdims=True))
    even = jnp.where(position < left, jnp.exp(even - top), 0.0).astype(bf16)
    odd = jnp.where(position + 1 < left, jnp.exp(odd - top), 0.0).astype(bf16)
    total = jnp.sum(even.astype(f32), axis=1, keepdims=True) + jnp.sum(odd.astype(f32), axis=1, keepdims=True)
    summed = dot(even, keys[:, :LATENT]) + dot(odd, keys[:, 512:])[:, 64 : 64 + LATENT]
    lane = lax.broadcasted_iota(jnp.int32, (128, 128), 1)
    stats = jnp.zeros((128, 128), f32)
    for at, piece in enumerate(pieces(top) + pieces(total)):
        stats = jnp.where(lane == at, piece, stats)
    found[:, :LATENT] = summed.astype(bf16)
    found[:, LATENT:] = stats.astype(bf16)
    span = pl.ds(pl.multiple_of(row * 32, 32), 32)
    for d, p_ref in enumerate(p_refs):
        share = pl.multiple_of(jnp.bitwise_xor(info_ref[9], d) * 32, 32)
        p_ref[span, :] = found[pl.ds(share, 32), :]


def attend(store, asked, info):
    shape = (256, PART)
    return pl.pallas_call(
        attend_kernel,
        grid_spec=pltpu.PrefetchScalarGridSpec(
            num_scalar_prefetch=1,
            grid=(8,),
            in_specs=[
                pl.BlockSpec((1, 1, LP * KV), lambda i, info: (0, 0, i)),
                pl.BlockSpec((1, 128, PART), lambda i, info: (i, 0, 0)),
            ],
            out_specs=[pl.BlockSpec(shape, lambda i, info: (0, 0))] * 4,
            scratch_shapes=[
                pltpu.VMEM((LP * KV // 128, 128), f32),
                pltpu.VMEM((LP // 2, 2 * KV), bf16),
                pltpu.VMEM((128, PART), bf16),
            ],
        ),
        out_shape=[jax.ShapeDtypeStruct(shape, bf16)] * 4,
        compiler_params=pltpu.CompilerParams(vmem_limit_bytes=VM),
    )(info, store, asked)


def unpack_kernel(tp_ref, s_ref, p0_ref, p1_ref, p2_ref, p3_ref, w_ref, scr):
    step = pl.program_id(0)
    flat_rows(s_ref, scr)
    for d, p_ref in enumerate((p0_ref, p1_ref, p2_ref, p3_ref)):

        @pl.when(step // 2 == d)
        def _():
            for m in range(3):
                p_ref[:, 128 * m : 128 * m + 128] = scr[pl.ds(m, 448, stride=3), :].astype(bf16)

    @pl.when(step >= 8)
    def _():
        for m in range(14):
            at = 128 * (m % 5)
            w_ref[m // 5, :, at : at + 128] = scr[pl.ds(m, HD, stride=14), :].astype(bf16)
        w_ref[2, :, 512:640] = jnp.zeros((HD, 128), bf16)


def unpack(store, part):
    def block(i, tp):
        return 0, 0, jnp.where(i < 8, jnp.bitwise_xor(i // 2, tp[0]) + 4 * (i % 2), i)

    def piece(d):
        return pl.BlockSpec((448, 384), lambda i, tp: (jnp.clip(i - 2 * d, 0, 1), 0))

    return pl.pallas_call(
        unpack_kernel,
        grid_spec=pltpu.PrefetchScalarGridSpec(
            num_scalar_prefetch=1,
            grid=(12,),
            in_specs=[pl.BlockSpec((1, 1, DQ * HD), block)],
            out_specs=[piece(d) for d in range(4)]
            + [pl.BlockSpec((3, HD, PART), lambda i, tp: (0, jnp.maximum(i - 8, 0), 0))],
            scratch_shapes=[pltpu.VMEM((DQ * HD // 128, 128), f32)],
        ),
        out_shape=[jax.ShapeDtypeStruct((896, 384), bf16)] * 4 + [jax.ShapeDtypeStruct((3, 384, PART), bf16)],
        compiler_params=pltpu.CompilerParams(vmem_limit_bytes=VM),
    )(part.reshape(1).astype(jnp.int32), store)


def weights_kernel(p0_ref, p1_ref, p2_ref, p3_ref, w_ref):
    for half in range(2):
        for r in range(4):
            span = slice(HD * r, HD * r + HD)
            rows = slice(448 * half, 448 * half + 448)
            found = jnp.concatenate([p_ref[rows, span] for p_ref in (p0_ref, p1_ref, p2_ref, p3_ref)], axis=1)
            for b in range(7):
                w_ref[half, 256 * b + 64 * r : 256 * b + 64 * r + 64, :] = found[64 * b : 64 * b + 64]


def arrange(quarters):
    return pl.pallas_call(
        weights_kernel,
        out_shape=jax.ShapeDtypeStruct((2, DQ, 384), bf16),
        compiler_params=pltpu.CompilerParams(vmem_limit_bytes=VM),
    )(*quarters)


def join_kernel(p0_ref, p1_ref, p2_ref, p3_ref, out_ref):
    refs = (p0_ref, p1_ref, p2_ref, p3_ref)
    tops, totals = [], []
    for p_ref in refs:
        stats = p_ref[:, LATENT:].astype(f32)
        tops.append(stats[:, 0:1] + stats[:, 1:2] + stats[:, 2:3])
        totals.append(stats[:, 3:4] + stats[:, 4:5] + stats[:, 5:6])
    top = functools.reduce(jnp.maximum, tops)
    scales = [jnp.exp(own - top) for own in tops]
    total = sum(scale * own for scale, own in zip(scales, totals))
    scales = [scale / total for scale in scales]
    out_ref[:, :LATENT] = sum(
        scale * p_ref[:, :LATENT].astype(f32) for scale, p_ref in zip(scales, refs)
    ).astype(bf16)
    lane = lax.broadcasted_iota(jnp.int32, (256, 128), 1)
    stats = jnp.zeros((256, 128), f32)
    for at, piece in enumerate(pieces(top + jnp.log(total))):
        stats = jnp.where(lane == at, piece, stats)
    out_ref[:, LATENT:] = stats.astype(bf16)


def join(parts):
    return pl.pallas_call(
        join_kernel,
        out_shape=jax.ShapeDtypeStruct((256, PART), bf16),
        compiler_params=pltpu.CompilerParams(vmem_limit_bytes=VM),
    )(*parts)


def project_kernel(tp_ref, x_ref, w_ref, z_ref, scr, slab):
    count = x_ref.shape[0]
    scr[...] = x_ref[...].astype(f32).reshape(scr.shape)
    for c in range(CAP):
        for k in range(14):
            slab[:, 128 * k : 128 * k + 128] = scr[pl.ds(16 * c + k, count, stride=48), :].astype(bf16)
        for half in range(2):
            turned = dot(slab[...], w_ref[half]).T.astype(bf16)
            for d in range(4):
                z_ref[jnp.bitwise_xor(tp_ref[0], d), HD * half : HD * half + HD, 128 * c : 128 * c + 128] = turned[
                    HD * d : HD * d + HD
                ]


def project(part, arrived, weights):
    count = arrived.shape[0]
    return pl.pallas_call(
        project_kernel,
        in_specs=[pl.BlockSpec(memory_space=pltpu.SMEM)] + [pl.BlockSpec(memory_space=pltpu.VMEM)] * 2,
        out_shape=jax.ShapeDtypeStruct((4, 2 * HD, CAP * count), bf16),
        scratch_shapes=[pltpu.VMEM((count * 48, 128), f32), pltpu.VMEM((count, DQ), bf16)],
        compiler_params=pltpu.CompilerParams(vmem_limit_bytes=VM),
    )(part.reshape(1).astype(jnp.int32), arrived, weights)


def descend_kernel(h_ref, w0_ref, w1_ref, w2_ref, out_ref, scr, turned):
    count = out_ref.shape[0]
    result = jnp.zeros((CAP * count, PART), f32)
    for d, w_ref in enumerate((w0_ref, w1_ref, w2_ref)):
        for t in range(4):
            scr[HD * t : HD * t + HD, :] = h_ref[t, d]
        result = result + dot(scr[...], w_ref[...], ((0,), (0,)))
    for c in range(CAP):
        for m in range(5):
            turned[pl.ds(5 * c + m, count, stride=16), :] = result[count * c : count * c + count, 128 * m : 128 * m + 128]
    turned[pl.ds(15, count, stride=16), :] = jnp.zeros((count, 128), f32)
    out_ref[...] = turned[...].astype(bf16).reshape(out_ref.shape)


def descend(hidden, downs):
    count = hidden.shape[3] // CAP
    return pl.pallas_call(
        descend_kernel,
        out_shape=jax.ShapeDtypeStruct((count, 16, 128), bf16),
        scratch_shapes=[pltpu.VMEM((4 * HD, CAP * count), bf16), pltpu.VMEM((count * 16, 128), f32)],
        compiler_params=pltpu.CompilerParams(vmem_limit_bytes=VM),
    )(hidden, *downs)


def combine_kernel(a_ref, x_ref, out_ref, scr):
    count = x_ref.shape[0]
    scr[...] = x_ref[...].astype(f32).reshape(scr.shape)
    for m in range(5):
        result = jnp.zeros((96, 128), f32)
        for c in range(CAP):
            result = result + dot(a_ref[c], scr[pl.ds(5 * c + m, count, stride=16), :].astype(bf16))
        result = (result[:48] + result[48:]).astype(bf16)
        for j in range(3 if m < 4 else 2):
            at = 640 * j + 128 * m
            out_ref[:, at : at + 128] = result[16 * j : 16 * j + 16]


def combine(weight, result):
    return pl.pallas_call(
        combine_kernel,
        out_shape=jax.ShapeDtypeStruct((16, DQ), bf16),
        scratch_shapes=[pltpu.VMEM((result.shape[0] * 16, 128), f32)],
        compiler_params=pltpu.CompilerParams(vmem_limit_bytes=VM),
    )(weight, result)


def per_device(store, queries, new_latent, cached_len, rows, expert_ids, route_gates, capacity):
    groups = lax.axis_size("sec")
    servers = groups // 4
    place = lax.axis_index("sec")
    part = lax.axis_index("tp")
    serving = place < servers
    both = ("sec", "tp")
    core = part % 2

    experts = capacity.shape[1]
    labels = jnp.arange(experts, dtype=jnp.int32)
    match = expert_ids[:, :, None] == labels[None, None, :]
    hits = jnp.any(match, axis=1).astype(jnp.int32)
    gate_of = jnp.sum(jnp.where(match, route_gates[:, :, None], 0.0), axis=1)
    rank = jnp.cumsum(hits, axis=0) - hits
    keep = (hits == 1) & (rank < capacity[0][None, :])
    slots = jnp.arange(CAP, dtype=jnp.int32)
    pick = (keep[None] & (rank[None] == slots[:, None, None])).astype(f32)
    spread = jnp.pad(jnp.repeat(pick, 3, axis=2), ((0, 0), (0, 0), (servers, 0)))
    sel = jnp.swapaxes(spread, 1, 2).astype(bf16)
    outgoing = dispatch(sel, rows)
    arrived = lax.all_to_all(outgoing, "sec", split_axis=0, concat_axis=0, tiled=True)

    def across(value, d, first, last):
        return lax.ppermute(value, both, [(4 * q + t, 4 * q + (t ^ d)) for q in range(first, last) for t in range(4)])

    def sibling(value, step):
        return lax.ppermute(
            value,
            "sec",
            [(servers + 3 * e + j, servers + 3 * e + (j + step) % 3) for e in range(experts) for j in range(3)],
        )

    *quarters, down = unpack(store, part)
    quarters = [quarters[0]] + [across(quarters[d], d, servers, groups) for d in range(1, 4)]
    third = (place - servers) % 3
    downs = [lax.dynamic_index_in_dim(down, third, 0, keepdims=False)]
    for step in (1, 2):
        downs.append(sibling(lax.dynamic_index_in_dim(down, (third + step) % 3, 0, keepdims=False), step))
    weights = arrange(quarters)

    digits = jnp.stack([cached_len // 64, cached_len % 64], axis=1).astype(bf16)
    digits = jnp.pad(digits, ((0, 0), (0, PART - KV - 2)))
    asked = jnp.concatenate([queries, jnp.broadcast_to(digits[:, None, :], (2, 128, PART - KV))], axis=2)
    half = lax.dynamic_slice_in_dim(asked, core * 64, 64, 1)
    incoming = [half]
    for k in range(1, 4):
        incoming.append(lax.ppermute(half, "sec", [(k * servers + a, a) for a in range(servers)]))
    half = jnp.concatenate(incoming, axis=0)
    other = across(half, 1, 0, servers)
    asked = jnp.concatenate([jnp.where(core == 0, half, other), jnp.where(core == 0, other, half)], axis=1)
    lengths = asked[:, 0, KV].astype(jnp.int32) * 64 + asked[:, 0, KV + 1].astype(jnp.int32)
    info = jnp.concatenate([lengths, jnp.stack([part * LP, part]).astype(jnp.int32)])

    parts = lax.cond(
        serving, lambda: tuple(attend(store, asked, info)), lambda: (jnp.zeros((256, PART), bf16),) * 4
    )
    parts = [parts[0]] + [across(parts[d], d, 0, servers) for d in range(1, 4)]
    answer = lax.cond(serving, lambda: join(parts), lambda: jnp.zeros((256, PART), bf16))

    answer = answer.reshape(4, 64, PART)
    returned = answer[0]
    for k in range(1, 4):
        returned = returned + lax.ppermute(answer[k], "sec", [(a, k * servers + a) for a in range(servers)])
    mine = lax.dynamic_slice_in_dim(queries, part * 32, 32, 1)
    own = jnp.einsum("rhk,rk->rh", mine, new_latent, preferred_element_type=f32) * softmax_scale
    own = own[:, :, None]
    returned = returned.reshape(2, 32, PART).astype(f32)
    others = returned[:, :, 512:513] + returned[:, :, 513:514] + returned[:, :, 514:515]
    top = jnp.maximum(own, others)
    own, others = jnp.exp(own - top), jnp.exp(others - top)
    attended = (others * returned[:, :, :LATENT] + own * new_latent[:, None, :LATENT].astype(f32)) / (own + others)
    attended = attended.astype(bf16)

    partial = project(part, arrived, weights)
    partial = lax.all_to_all(partial, "tp", split_axis=0, concat_axis=0, tiled=True)
    partial = jnp.sum(partial.astype(f32), axis=0)
    hidden = (jax.nn.silu(partial[:HD]) * partial[HD:]).astype(bf16)
    hidden = jnp.stack([hidden, sibling(hidden, 1), sibling(hidden, 2)])
    hidden = lax.all_gather(hidden, "tp", axis=0)
    result = descend(hidden, downs)
    result = lax.all_to_all(result, "sec", split_axis=0, concat_axis=0, tiled=True)

    scaled = spread * jnp.pad(jnp.repeat(gate_of, 3, axis=1), ((0, 0), (servers, 0)))[None]
    holder = (jnp.arange(groups) - servers) % 3
    scaled = jnp.where(holder == jnp.arange(3)[:, None, None, None], scaled[None], 0.0)
    scaled = jnp.swapaxes(scaled, 0, 1).reshape(CAP, 48, groups)
    high = lax.reduce_precision(scaled, 8, 7)
    weight = jnp.concatenate([high, scaled - high], axis=1).astype(bf16)
    mixed = combine(weight, result)
    return (attended, mixed)


def solution(mesh):
    placed = (
        P("sec", "tp", None),
        P("sec", None, None),
        P("sec", None),
        P("sec"),
        P("sec", "tp"),
        P("sec", None),
        P("sec", None),
        P("sec", None),
    )
    return jax.shard_map(
        per_device,
        mesh=mesh,
        in_specs=placed,
        out_specs=(P("sec", "tp", None), P("sec", "tp")),
        check_vma=False,
    )
```

```python
import functools
import math

import jax
import jax.numpy as jnp
from jax import lax
from jax.experimental import pallas as pl
from jax.experimental.pallas import tpu as pltpu
from jax.sharding import PartitionSpec as P

LATENT = 512
KV = 576
LP = 512
CAP = 3
HD = 96
DQ = 1792
PART = 640
f32 = jnp.float32
bf16 = jnp.bfloat16
VM = 16 << 20

softmax_scale = 1.0 / math.sqrt(192.0)


whole = pl.BlockSpec(memory_space=pltpu.VMEM)
after = pl.BlockSpec(memory_space=pl.ANY)


def dot(a, b, dims=((1,), (0,))):
    return lax.dot_general(a, b, (dims, ((), ())), preferred_element_type=f32)


def pieces(value):
    high = value.astype(bf16).astype(f32)
    middle = (value - high).astype(bf16).astype(f32)
    return high, middle, value - high - middle


def flat_rows(s_ref, scr):
    scr[...] = s_ref[...].astype(f32).reshape(scr.shape)


def dispatch_kernel(sel_ref, rows_ref, *refs):
    out_ref, scr = refs[-2:]
    source = lax.broadcasted_iota(jnp.int32, (256, 256), 0)
    target = lax.broadcasted_iota(jnp.int32, (256, 256), 1)
    order = (source == 4 * (target % 64) + target // 64).astype(f32).astype(bf16)
    count = out_ref.shape[0]
    for b in range(DQ // 256):
        turned = dot(rows_ref[:, 256 * b : 256 * b + 256], order).astype(bf16)
        for c in range(CAP):
            sent = dot(sel_ref[c], turned)
            for k in range(2):
                scr[pl.ds(16 * c + 2 * b + k, count, stride=48), :] = sent[:, 128 * k : 128 * k + 128]
    for c in range(CAP):
        for k in range(14, 16):
            scr[pl.ds(16 * c + k, count, stride=48), :] = jnp.zeros((count, 128), f32)
    out_ref[...] = scr[...].astype(bf16).reshape(out_ref.shape)


def dispatch(sel, rows, *earlier):
    groups = sel.shape[1]
    return pl.pallas_call(
        dispatch_kernel,
        in_specs=[whole] * 2 + [after] * len(earlier),
        out_shape=jax.ShapeDtypeStruct((groups, 48, 128), bf16),
        scratch_shapes=[pltpu.VMEM((groups * 48, 128), f32)],
        compiler_params=pltpu.CompilerParams(vmem_limit_bytes=VM),
    )(sel, rows, *earlier)


def ask_kernel(tp_ref, length_ref, q_ref, out_ref):
    out_ref[:KV] = q_ref[0]
    length = length_ref[tp_ref[0] % 2]
    row = lax.broadcasted_iota(jnp.int32, (16, 128), 0)
    out_ref[KV:] = jnp.where(row == 0, length // 64, length % 64).astype(f32).astype(bf16)


def ask(part, lengths, queries):
    return pl.pallas_call(
        ask_kernel,
        grid_spec=pltpu.PrefetchScalarGridSpec(
            num_scalar_prefetch=2,
            grid=(1,),
            in_specs=[pl.BlockSpec((1, KV, 128), lambda i, tp, lengths: (tp[0] % 2, 0, 0))],
            out_specs=pl.BlockSpec((KV + 16, 128), lambda i, tp, lengths: (0, 0)),
        ),
        out_shape=jax.ShapeDtypeStruct((KV + 16, 128), bf16),
    )(part.reshape(1).astype(jnp.int32), lengths, queries)


def stack_kernel(*refs):
    for n in range(4):
        refs[-1][n] = refs[n][...]


def stack(rows, earlier):
    return pl.pallas_call(
        stack_kernel,
        in_specs=[whole] * 4 + [after],
        out_shape=jax.ShapeDtypeStruct((4,) + rows[0].shape, bf16),
    )(*rows, earlier)


def attend_kernel(tp_ref, s_ref, mine_ref, other_ref, *refs):
    p_refs, (scr, keys, found) = refs[:4], refs[4:]
    step = pl.program_id(0)
    row = served(step, tp_ref)
    flat_rows(s_ref, scr)
    for m in range(9):
        keys[:, 128 * m : 128 * m + 128] = scr[pl.ds(m, LP // 2, stride=9), :].astype(bf16)
    asked = jnp.where(step < 4, mine_ref[0].astype(f32), other_ref[0].astype(f32))
    left = asked[KV : KV + 1, 0:1] * 64.0 + asked[KV + 1 : KV + 2, 0:1] - (tp_ref[0] * LP).astype(f32)
    gap = jnp.zeros((64, 128), f32)
    even_q = jnp.concatenate([asked[:KV], gap], axis=0).T.astype(bf16)
    odd_q = jnp.concatenate([gap, asked[:KV]], axis=0).T.astype(bf16)
    even = dot(even_q, keys[:, :640], ((1,), (1,))) * softmax_scale
    odd = dot(odd_q, keys[:, 512:], ((1,), (1,))) * softmax_scale
    position = (2 * lax.broadcasted_iota(jnp.int32, (128, LP // 2), 1)).astype(f32)
    even = jnp.where(position < left, even, -1e30)
    odd = jnp.where(position + 1.0 < left, odd, -1e30)
    top = jnp.maximum(jnp.max(even, axis=1, keepdims=True), jnp.max(odd, axis=1, keepdims=True))
    even = jnp.where(position < left, jnp.exp(even - top), 0.0).astype(bf16)
    odd = jnp.where(position + 1.0 < left, jnp.exp(odd - top), 0.0).astype(bf16)
    total = jnp.sum(even.astype(f32), axis=1, keepdims=True) + jnp.sum(odd.astype(f32), axis=1, keepdims=True)
    summed = dot(even, keys[:, :LATENT]) + dot(odd, keys[:, 512:])[:, 64 : 64 + LATENT]
    lane = lax.broadcasted_iota(jnp.int32, (128, 128), 1)
    stats = jnp.zeros((128, 128), f32)
    for at, piece in enumerate(pieces(top) + pieces(total)):
        stats = jnp.where(lane == at, piece, stats)
    found[:, :LATENT] = summed.astype(bf16)
    found[:, LATENT:] = stats.astype(bf16)
    span = pl.ds(pl.multiple_of(row * 32, 32), 32)
    for d, p_ref in enumerate(p_refs):
        share = pl.multiple_of(jnp.bitwise_xor(tp_ref[0], d) * 32, 32)
        p_ref[span, :] = found[pl.ds(share, 32), :]


def served(step, tp):
    return 2 * (step % 4) + jnp.bitwise_xor(tp[0] % 2, step // 4)


def attend(store, mine, other, part):
    shape = (256, PART)
    rows = (1,) + mine.shape[1:]
    return pl.pallas_call(
        attend_kernel,
        grid_spec=pltpu.PrefetchScalarGridSpec(
            num_scalar_prefetch=1,
            grid=(8,),
            in_specs=[
                pl.BlockSpec((1, 1, LP * KV), lambda i, tp: (0, 0, served(i, tp))),
                pl.BlockSpec(rows, lambda i, tp: (jnp.minimum(i, 3), 0, 0)),
                pl.BlockSpec(rows, lambda i, tp: (jnp.maximum(i - 4, 0), 0, 0)),
            ],
            out_specs=[pl.BlockSpec(shape, lambda i, tp: (0, 0))] * 4,
            scratch_shapes=[
                pltpu.VMEM((LP * KV // 128, 128), f32),
                pltpu.VMEM((LP // 2, 2 * KV), bf16),
                pltpu.VMEM((128, PART), bf16),
            ],
        ),
        out_shape=[jax.ShapeDtypeStruct(shape, bf16)] * 4,
        compiler_params=pltpu.CompilerParams(vmem_limit_bytes=VM),
    )(part.reshape(1).astype(jnp.int32), store, mine, other)


def unpack_kernel(tp_ref, s_ref, _, p_ref, *refs):
    scr = refs[-1]
    step = pl.program_id(0)
    flat_rows(s_ref, scr)

    @pl.when(step < 4)
    def _():
        for m in range(3):
            p_ref[:, 128 * m : 128 * m + 128] = scr[pl.ds(m, 448, stride=3), :].astype(bf16)

    if len(refs) > 1:
        w_ref = refs[0]

        @pl.when(step >= 4)
        def _():
            for m in range(14):
                w_ref[:, 128 * m : 128 * m + 128] = scr[pl.ds(m, HD, stride=14), :].astype(bf16)


def unpack(store, part, far, earlier):
    def block(i, tp):
        x_hi = jnp.bitwise_xor(tp[0] // 2, 1 if far else 0)
        return 0, 0, jnp.where(i < 4, 4 * (i // 2) + 2 * x_hi + i % 2, i + 4)

    out_specs = [pl.BlockSpec((448, 384), lambda i, tp: (jnp.minimum(i, 3), 0))]
    out_shape = [jax.ShapeDtypeStruct((DQ, 384), bf16)]
    if not far:
        out_specs.append(pl.BlockSpec((HD, DQ), lambda i, tp: (jnp.maximum(i - 4, 0), 0)))
        out_shape.append(jax.ShapeDtypeStruct((4 * HD, DQ), bf16))
    return pl.pallas_call(
        unpack_kernel,
        grid_spec=pltpu.PrefetchScalarGridSpec(
            num_scalar_prefetch=1,
            grid=(4 if far else 8,),
            in_specs=[pl.BlockSpec((1, 1, DQ * HD), block), after],
            out_specs=out_specs,
            scratch_shapes=[pltpu.VMEM((DQ * HD // 128, 128), f32)],
        ),
        out_shape=out_shape,
        compiler_params=pltpu.CompilerParams(vmem_limit_bytes=VM),
    )(part.reshape(1).astype(jnp.int32), store, earlier)


def weights_kernel(tp_ref, here_ref, far_ref, w_ref, mark_ref):
    mark_ref[...] = jnp.zeros_like(mark_ref)

    def fill(refs):
        for half in range(2):
            for q in range(2):
                rows = slice(896 * half + 448 * q, 896 * half + 448 * q + 448)
                for r in range(4):
                    found = jnp.concatenate([ref[rows, HD * r : HD * r + HD] for ref in refs], axis=1)
                    for b in range(7):
                        at = DQ * q + 256 * b + 64 * r
                        w_ref[half, at : at + 64, :] = found[64 * b : 64 * b + 64]

    @pl.when(tp_ref[0] < 2)
    def _():
        fill((here_ref, far_ref))

    @pl.when(tp_ref[0] >= 2)
    def _():
        fill((far_ref, here_ref))


def arrange(part, here, far):
    return pl.pallas_call(
        weights_kernel,
        in_specs=[pl.BlockSpec(memory_space=pltpu.SMEM), whole, whole],
        out_shape=[jax.ShapeDtypeStruct((2, 2 * DQ, 2 * HD), bf16), jax.ShapeDtypeStruct((8, 128), f32)],
        compiler_params=pltpu.CompilerParams(vmem_limit_bytes=VM),
    )(part.reshape(1).astype(jnp.int32), here, far)


def join_kernel(p0_ref, p1_ref, p2_ref, p3_ref, out_ref):
    refs = (p0_ref, p1_ref, p2_ref, p3_ref)
    tops, totals = [], []
    for p_ref in refs:
        stats = p_ref[:, LATENT:].astype(f32)
        tops.append(stats[:, 0:1] + stats[:, 1:2] + stats[:, 2:3])
        totals.append(stats[:, 3:4] + stats[:, 4:5] + stats[:, 5:6])
    top = functools.reduce(jnp.maximum, tops)
    scales = [jnp.exp(own - top) for own in tops]
    total = sum(scale * own for scale, own in zip(scales, totals))
    scales = [scale / total for scale in scales]
    out_ref[:, :LATENT] = sum(
        scale * p_ref[:, :LATENT].astype(f32) for scale, p_ref in zip(scales, refs)
    ).astype(bf16)
    lane = lax.broadcasted_iota(jnp.int32, (256, 128), 1)
    stats = jnp.zeros((256, 128), f32)
    for at, piece in enumerate(pieces(top + jnp.log(total))):
        stats = jnp.where(lane == at, piece, stats)
    out_ref[:, LATENT:] = stats.astype(bf16)


def join(parts):
    return pl.pallas_call(
        join_kernel,
        out_shape=jax.ShapeDtypeStruct((256, PART), bf16),
        compiler_params=pltpu.CompilerParams(vmem_limit_bytes=VM),
    )(*parts)


def slab_kernel(x_ref, *refs):
    out_ref, scr = refs[-2:]
    count = x_ref.shape[0]
    scr[...] = x_ref[...].astype(f32).reshape(scr.shape)
    for c in range(CAP):
        for k in range(14):
            found = scr[pl.ds(16 * c + k, count, stride=48), :].astype(bf16)
            out_ref[count * c : count * c + count, 128 * k : 128 * k + 128] = found


def slots_of(arrived, *earlier):
    count = arrived.shape[0]
    return pl.pallas_call(
        slab_kernel,
        in_specs=[whole] + [after] * len(earlier),
        out_shape=jax.ShapeDtypeStruct((CAP * count, DQ), bf16),
        scratch_shapes=[pltpu.VMEM((count * 48, 128), f32)],
        compiler_params=pltpu.CompilerParams(vmem_limit_bytes=VM),
    )(arrived, *earlier)


def project_kernel(_, x_ref, w_ref, *refs):
    z_ref = refs[-1]
    for half in range(2):
        found = dot(x_ref[...], w_ref[half])
        if len(refs) > 1:
            found = found + refs[0][half]
            z_ref[2 * HD * half : 2 * HD * half + 2 * HD, :] = found.T.astype(bf16)
        else:
            z_ref[half] = found


def project(core, slab, weights, *other):
    slots = slab.shape[0]
    if other:
        shape = jax.ShapeDtypeStruct((4 * HD, slots), bf16)
    else:
        shape = jax.ShapeDtypeStruct((2, slots, 2 * HD), f32)
    full = lambda array: pl.BlockSpec(array.shape, lambda i, core: (0,) * len(array.shape))
    return pl.pallas_call(
        project_kernel,
        grid_spec=pltpu.PrefetchScalarGridSpec(
            num_scalar_prefetch=1,
            grid=(1,),
            in_specs=[full(slab), pl.BlockSpec((2, DQ, 2 * HD), lambda i, core: (0, core[0], 0))]
            + [full(sums) for sums in other],
            out_specs=full(shape),
        ),
        out_shape=shape,
        compiler_params=pltpu.CompilerParams(vmem_limit_bytes=VM),
    )(core.reshape(1).astype(jnp.int32), slab, weights, *other)


def descend_kernel(core_ref, h_ref, o_ref, w_ref, out_ref, scr, turned):
    count = out_ref.shape[0]
    core = core_ref[0]
    for x_hi in range(2):
        rows = slice(HD * x_hi, HD * x_hi + HD)
        for at, ref in ((2 * x_hi + core, h_ref), (2 * x_hi + 1 - core, o_ref)):
            scr[pl.ds(pl.multiple_of(at * HD, HD), HD), :] = ref[rows]
    for c in range(CAP):
        result = dot(scr[:, count * c : count * c + count], w_ref[...], ((0,), (0,)))
        for k in range(14):
            turned[pl.ds(16 * c + k, count, stride=48), :] = result[:, 128 * k : 128 * k + 128]
        for k in range(14, 16):
            turned[pl.ds(16 * c + k, count, stride=48), :] = jnp.zeros((count, 128), f32)
    out_ref[...] = turned[...].astype(bf16).reshape(out_ref.shape)


def descend(core, hidden, other, down):
    count = hidden.shape[1] // CAP
    return pl.pallas_call(
        descend_kernel,
        in_specs=[pl.BlockSpec(memory_space=pltpu.SMEM)] + [whole] * 3,
        out_shape=jax.ShapeDtypeStruct((count, 48, 128), bf16),
        scratch_shapes=[pltpu.VMEM((4 * HD, CAP * count), bf16), pltpu.VMEM((count * 48, 128), f32)],
        compiler_params=pltpu.CompilerParams(vmem_limit_bytes=VM),
    )(core.reshape(1).astype(jnp.int32), hidden, other, down)


def combine_kernel(a_ref, x_ref, out_ref, scr):
    count = x_ref.shape[0]
    scr[...] = x_ref[...].astype(f32).reshape(scr.shape)
    for k in range(14):
        result = jnp.zeros((32, 128), f32)
        for c in range(CAP):
            result = result + dot(a_ref[c], scr[pl.ds(16 * c + k, count, stride=48), :].astype(bf16))
        out_ref[:, 128 * k : 128 * k + 128] = (result[:16] + result[16:]).astype(bf16)


def combine(weight, result):
    return pl.pallas_call(
        combine_kernel,
        out_shape=jax.ShapeDtypeStruct((16, DQ), bf16),
        scratch_shapes=[pltpu.VMEM((result.shape[0] * 48, 128), f32)],
        compiler_params=pltpu.CompilerParams(vmem_limit_bytes=VM),
    )(weight, result)


def per_device(store, queries, new_latent, cached_len, rows, expert_ids, route_gates, capacity):
    groups = lax.axis_size("sec")
    servers = groups // 4
    place = lax.axis_index("sec")
    part = lax.axis_index("tp")
    serving = place < servers
    both = ("sec", "tp")
    core = part % 2
    experts = capacity.shape[1]

    def across(value, d, first, last):
        return lax.ppermute(value, both, [(4 * q + t, 4 * q + (t ^ d)) for q in range(first, last) for t in range(4)])

    labels = jnp.arange(experts, dtype=jnp.int32)
    match = expert_ids[:, :, None] == labels[None, None, :]
    hits = jnp.any(match, axis=1).astype(jnp.int32)
    gate_of = jnp.sum(jnp.where(match, route_gates[:, :, None], 0.0), axis=1)
    rank = jnp.cumsum(hits, axis=0) - hits
    keep = (hits == 1) & (rank < capacity[0][None, :])
    slots = jnp.arange(CAP, dtype=jnp.int32)
    pick = (keep[None] & (rank[None] == slots[:, None, None])).astype(f32)
    spread = jnp.pad(jnp.repeat(pick, 3, axis=2), ((0, 0), (0, 0), (servers, 0)))
    sel = jnp.swapaxes(spread, 1, 2).astype(bf16)

    asked = ask(part, cached_len, jnp.swapaxes(queries, 1, 2))
    mine = [asked]
    for k in range(1, 4):
        mine.append(lax.ppermute(asked, "sec", [(k * servers + a, a) for a in range(servers)]))
    outgoing = dispatch(sel, rows)
    mine = stack(mine, outgoing[0, :16])
    (far,) = unpack(store, part, True, mine[0, :16])
    far = across(far, 2, servers, groups)

    def window():
        arrived = lax.all_to_all(outgoing, "sec", split_axis=0, concat_axis=0, tiled=True)
        other = across(mine, 1, 0, servers)
        here, down = unpack(store, part, False, outgoing[0, :16])
        parts = lax.cond(
            serving,
            lambda: tuple(attend(store, mine, other, part)),
            lambda: (jnp.zeros((256, PART), bf16),) * 4,
        )
        parts = [parts[0]] + [across(parts[d], d, 0, servers) for d in range(1, 4)]
        answer = lax.cond(serving, lambda: join(parts), lambda: jnp.zeros((256, PART), bf16))
        return arrived, here, down, answer

    def experts_part():
        slab = slots_of(arrived)
        beside = across(slab, 1, servers, groups)
        partial = project(core, slab, weights)
        partial = project(1 - core, beside, weights, partial)
        partial = partial.astype(f32) + across(partial, 2, servers, groups).astype(f32)
        hidden = (jax.nn.silu(partial[: 2 * HD]) * partial[2 * HD :]).astype(bf16)
        return descend(core, hidden, across(hidden, 1, servers, groups), down)

    def way_back():
        back = lax.all_to_all(result, "sec", split_axis=0, concat_axis=0, tiled=True)
        shares = answer.reshape(4, 64, PART)
        returned = shares[0]
        for k in range(1, 4):
            returned = returned + lax.ppermute(shares[k], "sec", [(a, k * servers + a) for a in range(servers)])
        mine = lax.dynamic_slice_in_dim(queries, part * 32, 32, 1)
        own = jnp.einsum("rhk,rk->rh", mine, new_latent, preferred_element_type=f32) * softmax_scale
        own = own[:, :, None]
        returned = returned.reshape(2, 32, PART).astype(f32)
        others = returned[:, :, 512:513] + returned[:, :, 513:514] + returned[:, :, 514:515]
        top = jnp.maximum(own, others)
        own, others = jnp.exp(own - top), jnp.exp(others - top)
        attended = (others * returned[:, :, :LATENT] + own * new_latent[:, None, :LATENT].astype(f32)) / (own + others)

        scaled = spread * jnp.pad(jnp.repeat(gate_of, 3, axis=1), ((0, 0), (servers, 0)))[None]
        high = lax.reduce_precision(scaled, 8, 7)
        weight = jnp.concatenate([high, scaled - high], axis=1).astype(bf16)
        return combine(weight, back), attended.astype(bf16)

    def held(steps):
        shapes = jax.eval_shape(steps)
        return lax.cond(
            capacity[0, 0] >= 0, steps, lambda: jax.tree.map(lambda leaf: jnp.zeros(leaf.shape, leaf.dtype), shapes)
        )

    arrived, here, down, answer = held(window)
    weights, _ = arrange(part, here, far)
    result = held(experts_part)
    mixed, attended = held(way_back)

    return (attended, mixed)


def solution(mesh):
    placed = (
        P("sec", "tp", None),
        P("sec", None, None),
        P("sec", None),
        P("sec"),
        P("sec", "tp"),
        P("sec", None),
        P("sec", None),
        P("sec", None),
    )
    return jax.shard_map(
        per_device,
        mesh=mesh,
        in_specs=placed,
        out_specs=(P("sec", "tp", None), P("sec", "tp")),
        check_vma=False,
    )
```

```python
import functools
import math

import jax
import jax.numpy as jnp
from jax import lax
from jax.experimental import pallas as pl
from jax.experimental.pallas import tpu as pltpu
from jax.sharding import PartitionSpec as P

LATENT = 512
KV = 576
LP = 512
CAP = 3
HD = 96
DQ = 1792
PART = 640
f32 = jnp.float32
bf16 = jnp.bfloat16
VM = 16 << 20

softmax_scale = 1.0 / math.sqrt(192.0)


whole = pl.BlockSpec(memory_space=pltpu.VMEM)
after = pl.BlockSpec(memory_space=pl.ANY)


def dot(a, b, dims=((1,), (0,))):
    return lax.dot_general(a, b, (dims, ((), ())), preferred_element_type=f32)


def pieces(value):
    high = value.astype(bf16).astype(f32)
    middle = (value - high).astype(bf16).astype(f32)
    return high, middle, value - high - middle


def flat_rows(s_ref, scr):
    scr[...] = s_ref[...].astype(f32).reshape(scr.shape)


def dispatch_kernel(sel_ref, rows_ref, *refs):
    out_ref, scr = refs[-2:]
    source = lax.broadcasted_iota(jnp.int32, (256, 256), 0)
    target = lax.broadcasted_iota(jnp.int32, (256, 256), 1)
    order = (source == 4 * (target % 64) + target // 64).astype(f32).astype(bf16)
    count = out_ref.shape[0]
    for b in range(DQ // 256):
        turned = dot(rows_ref[:, 256 * b : 256 * b + 256], order).astype(bf16)
        for c in range(CAP):
            sent = dot(sel_ref[c], turned)
            for k in range(2):
                scr[pl.ds(16 * c + 2 * b + k, count, stride=48), :] = sent[:, 128 * k : 128 * k + 128]
    for c in range(CAP):
        for k in range(14, 16):
            scr[pl.ds(16 * c + k, count, stride=48), :] = jnp.zeros((count, 128), f32)
    out_ref[...] = scr[...].astype(bf16).reshape(out_ref.shape)


def dispatch(sel, rows, *earlier):
    groups = sel.shape[1]
    return pl.pallas_call(
        dispatch_kernel,
        in_specs=[whole] * 2 + [after] * len(earlier),
        out_shape=jax.ShapeDtypeStruct((groups, 48, 128), bf16),
        scratch_shapes=[pltpu.VMEM((groups * 48, 128), f32)],
        compiler_params=pltpu.CompilerParams(vmem_limit_bytes=VM),
    )(sel, rows, *earlier)


def ask_kernel(tp_ref, length_ref, q_ref, out_ref):
    out_ref[:KV] = q_ref[0]
    length = length_ref[tp_ref[0] % 2]
    row = lax.broadcasted_iota(jnp.int32, (16, 128), 0)
    out_ref[KV:] = jnp.where(row == 0, length // 64, length % 64).astype(f32).astype(bf16)


def ask(part, lengths, queries):
    return pl.pallas_call(
        ask_kernel,
        grid_spec=pltpu.PrefetchScalarGridSpec(
            num_scalar_prefetch=2,
            grid=(1,),
            in_specs=[pl.BlockSpec((1, KV, 128), lambda i, tp, lengths: (tp[0] % 2, 0, 0))],
            out_specs=pl.BlockSpec((KV + 16, 128), lambda i, tp, lengths: (0, 0)),
        ),
        out_shape=jax.ShapeDtypeStruct((KV + 16, 128), bf16),
    )(part.reshape(1).astype(jnp.int32), lengths, queries)


def stack_kernel(*refs):
    for n in range(4):
        refs[-1][n] = refs[n][...]


def stack(rows, earlier):
    return pl.pallas_call(
        stack_kernel,
        in_specs=[whole] * 4 + [after],
        out_shape=jax.ShapeDtypeStruct((4,) + rows[0].shape, bf16),
    )(*rows, earlier)


def attend_kernel(tp_ref, s_ref, mine_ref, other_ref, *refs):
    p_refs, (scr, keys, found) = refs[:4], refs[4:]
    step = pl.program_id(0)
    row = served(step, tp_ref)
    flat_rows(s_ref, scr)
    for m in range(9):
        keys[:, 128 * m : 128 * m + 128] = scr[pl.ds(m, LP // 2, stride=9), :].astype(bf16)
    asked = jnp.where(step < 4, mine_ref[0].astype(f32), other_ref[0].astype(f32))
    left = asked[KV : KV + 1, 0:1] * 64.0 + asked[KV + 1 : KV + 2, 0:1] - (tp_ref[0] * LP).astype(f32)
    gap = jnp.zeros((64, 128), f32)
    even_q = jnp.concatenate([asked[:KV], gap], axis=0).T.astype(bf16)
    odd_q = jnp.concatenate([gap, asked[:KV]], axis=0).T.astype(bf16)
    even = dot(even_q, keys[:, :640], ((1,), (1,))) * softmax_scale
    odd = dot(odd_q, keys[:, 512:], ((1,), (1,))) * softmax_scale
    position = (2 * lax.broadcasted_iota(jnp.int32, (128, LP // 2), 1)).astype(f32)
    even = jnp.where(position < left, even, -1e30)
    odd = jnp.where(position + 1.0 < left, odd, -1e30)
    top = jnp.maximum(jnp.max(even, axis=1, keepdims=True), jnp.max(odd, axis=1, keepdims=True))
    even = jnp.where(position < left, jnp.exp(even - top), 0.0).astype(bf16)
    odd = jnp.where(position + 1.0 < left, jnp.exp(odd - top), 0.0).astype(bf16)
    total = jnp.sum(even.astype(f32), axis=1, keepdims=True) + jnp.sum(odd.astype(f32), axis=1, keepdims=True)
    summed = dot(even, keys[:, :LATENT]) + dot(odd, keys[:, 512:])[:, 64 : 64 + LATENT]
    lane = lax.broadcasted_iota(jnp.int32, (128, 128), 1)
    stats = jnp.zeros((128, 128), f32)
    for at, piece in enumerate(pieces(top) + pieces(total)):
        stats = jnp.where(lane == at, piece, stats)
    found[:, :LATENT] = summed.astype(bf16)
    found[:, LATENT:] = stats.astype(bf16)
    span = pl.ds(pl.multiple_of(row * 32, 32), 32)
    for d, p_ref in enumerate(p_refs):
        share = pl.multiple_of(jnp.bitwise_xor(tp_ref[0], d) * 32, 32)
        p_ref[span, :] = found[pl.ds(share, 32), :]


def served(step, tp):
    return 2 * (step % 4) + jnp.bitwise_xor(tp[0] % 2, step // 4)


def attend(store, mine, other, part):
    shape = (256, PART)
    rows = (1,) + mine.shape[1:]
    return pl.pallas_call(
        attend_kernel,
        grid_spec=pltpu.PrefetchScalarGridSpec(
            num_scalar_prefetch=1,
            grid=(8,),
            in_specs=[
                pl.BlockSpec((1, 1, LP * KV), lambda i, tp: (0, 0, served(i, tp))),
                pl.BlockSpec(rows, lambda i, tp: (jnp.minimum(i, 3), 0, 0)),
                pl.BlockSpec(rows, lambda i, tp: (jnp.maximum(i - 4, 0), 0, 0)),
            ],
            out_specs=[pl.BlockSpec(shape, lambda i, tp: (0, 0))] * 4,
            scratch_shapes=[
                pltpu.VMEM((LP * KV // 128, 128), f32),
                pltpu.VMEM((LP // 2, 2 * KV), bf16),
                pltpu.VMEM((128, PART), bf16),
            ],
        ),
        out_shape=[jax.ShapeDtypeStruct(shape, bf16)] * 4,
        compiler_params=pltpu.CompilerParams(vmem_limit_bytes=VM),
    )(part.reshape(1).astype(jnp.int32), store, mine, other)


def unpack_kernel(tp_ref, s_ref, _, p_ref, *refs):
    scr = refs[-1]
    step = pl.program_id(0)
    flat_rows(s_ref, scr)

    @pl.when(step < 4)
    def _():
        for m in range(3):
            p_ref[:, 128 * m : 128 * m + 128] = scr[pl.ds(m, 448, stride=3), :].astype(bf16)

    if len(refs) > 1:
        w_ref = refs[0]

        @pl.when(step >= 4)
        def _():
            for m in range(14):
                w_ref[:, 128 * m : 128 * m + 128] = scr[pl.ds(m, HD, stride=14), :].astype(bf16)


def unpack(store, part, far, earlier):
    def block(i, tp):
        x_hi = jnp.bitwise_xor(tp[0] // 2, 1 if far else 0)
        return 0, 0, jnp.where(i < 4, 4 * (i // 2) + 2 * x_hi + i % 2, i + 4)

    out_specs = [pl.BlockSpec((448, 384), lambda i, tp: (jnp.minimum(i, 3), 0))]
    out_shape = [jax.ShapeDtypeStruct((DQ, 384), bf16)]
    if not far:
        out_specs.append(pl.BlockSpec((HD, DQ), lambda i, tp: (jnp.maximum(i - 4, 0), 0)))
        out_shape.append(jax.ShapeDtypeStruct((4 * HD, DQ), bf16))
    return pl.pallas_call(
        unpack_kernel,
        grid_spec=pltpu.PrefetchScalarGridSpec(
            num_scalar_prefetch=1,
            grid=(4 if far else 8,),
            in_specs=[pl.BlockSpec((1, 1, DQ * HD), block), after],
            out_specs=out_specs,
            scratch_shapes=[pltpu.VMEM((DQ * HD // 128, 128), f32)],
        ),
        out_shape=out_shape,
        compiler_params=pltpu.CompilerParams(vmem_limit_bytes=VM),
    )(part.reshape(1).astype(jnp.int32), store, earlier)


def weights_kernel(tp_ref, here_ref, far_ref, _, w_ref, mark_ref):
    mark_ref[...] = jnp.zeros_like(mark_ref)

    def fill(refs):
        for half in range(2):
            for q in range(2):
                rows = slice(896 * half + 448 * q, 896 * half + 448 * q + 448)
                for r in range(4):
                    found = jnp.concatenate([ref[rows, HD * r : HD * r + HD] for ref in refs], axis=1)
                    for b in range(7):
                        at = DQ * q + 256 * b + 64 * r
                        w_ref[half, at : at + 64, :] = found[64 * b : 64 * b + 64]

    @pl.when(tp_ref[0] < 2)
    def _():
        fill((here_ref, far_ref))

    @pl.when(tp_ref[0] >= 2)
    def _():
        fill((far_ref, here_ref))


def arrange(part, here, far, earlier):
    return pl.pallas_call(
        weights_kernel,
        in_specs=[pl.BlockSpec(memory_space=pltpu.SMEM), whole, whole, after],
        out_shape=[jax.ShapeDtypeStruct((2, 2 * DQ, 2 * HD), bf16), jax.ShapeDtypeStruct((8, 128), f32)],
        compiler_params=pltpu.CompilerParams(vmem_limit_bytes=VM),
    )(part.reshape(1).astype(jnp.int32), here, far, earlier)


def join_kernel(p0_ref, p1_ref, p2_ref, p3_ref, out_ref):
    refs = (p0_ref, p1_ref, p2_ref, p3_ref)
    tops, totals = [], []
    for p_ref in refs:
        stats = p_ref[:, LATENT:].astype(f32)
        tops.append(stats[:, 0:1] + stats[:, 1:2] + stats[:, 2:3])
        totals.append(stats[:, 3:4] + stats[:, 4:5] + stats[:, 5:6])
    top = functools.reduce(jnp.maximum, tops)
    scales = [jnp.exp(own - top) for own in tops]
    total = sum(scale * own for scale, own in zip(scales, totals))
    scales = [scale / total for scale in scales]
    out_ref[:, :LATENT] = sum(
        scale * p_ref[:, :LATENT].astype(f32) for scale, p_ref in zip(scales, refs)
    ).astype(bf16)
    lane = lax.broadcasted_iota(jnp.int32, (256, 128), 1)
    stats = jnp.zeros((256, 128), f32)
    for at, piece in enumerate(pieces(top + jnp.log(total))):
        stats = jnp.where(lane == at, piece, stats)
    out_ref[:, LATENT:] = stats.astype(bf16)


def join(parts):
    return pl.pallas_call(
        join_kernel,
        out_shape=jax.ShapeDtypeStruct((256, PART), bf16),
        compiler_params=pltpu.CompilerParams(vmem_limit_bytes=VM),
    )(*parts)


def slab_kernel(x_ref, *refs):
    out_ref, scr = refs[-2:]
    count = x_ref.shape[0]
    scr[...] = x_ref[...].astype(f32).reshape(scr.shape)
    for c in range(CAP):
        for k in range(14):
            found = scr[pl.ds(16 * c + k, count, stride=48), :].astype(bf16)
            out_ref[count * c : count * c + count, 128 * k : 128 * k + 128] = found


def slots_of(arrived, *earlier):
    count = arrived.shape[0]
    return pl.pallas_call(
        slab_kernel,
        in_specs=[whole] + [after] * len(earlier),
        out_shape=jax.ShapeDtypeStruct((CAP * count, DQ), bf16),
        scratch_shapes=[pltpu.VMEM((count * 48, 128), f32)],
        compiler_params=pltpu.CompilerParams(vmem_limit_bytes=VM),
    )(arrived, *earlier)


def project_kernel(_, x_ref, w_ref, *refs):
    z_ref = refs[-1]
    for half in range(2):
        found = dot(x_ref[...], w_ref[half])
        if len(refs) > 1:
            found = found + refs[0][half]
            z_ref[2 * HD * half : 2 * HD * half + 2 * HD, :] = found.T.astype(bf16)
        else:
            z_ref[half] = found


def project(core, slab, weights, *other):
    slots = slab.shape[0]
    if other:
        shape = jax.ShapeDtypeStruct((4 * HD, slots), bf16)
    else:
        shape = jax.ShapeDtypeStruct((2, slots, 2 * HD), f32)
    full = lambda array: pl.BlockSpec(array.shape, lambda i, core: (0,) * len(array.shape))
    return pl.pallas_call(
        project_kernel,
        grid_spec=pltpu.PrefetchScalarGridSpec(
            num_scalar_prefetch=1,
            grid=(1,),
            in_specs=[full(slab), pl.BlockSpec((2, DQ, 2 * HD), lambda i, core: (0, core[0], 0))]
            + [full(sums) for sums in other],
            out_specs=full(shape),
        ),
        out_shape=shape,
        compiler_params=pltpu.CompilerParams(vmem_limit_bytes=VM),
    )(core.reshape(1).astype(jnp.int32), slab, weights, *other)


def descend_kernel(core_ref, h_ref, o_ref, w_ref, out_ref, scr, turned):
    count = out_ref.shape[0]
    core = core_ref[0]
    for x_hi in range(2):
        rows = slice(HD * x_hi, HD * x_hi + HD)
        for at, ref in ((2 * x_hi + core, h_ref), (2 * x_hi + 1 - core, o_ref)):
            scr[pl.ds(pl.multiple_of(at * HD, HD), HD), :] = ref[rows]
    for c in range(CAP):
        result = dot(scr[:, count * c : count * c + count], w_ref[...], ((0,), (0,)))
        for k in range(14):
            turned[pl.ds(16 * c + k, count, stride=48), :] = result[:, 128 * k : 128 * k + 128]
        for k in range(14, 16):
            turned[pl.ds(16 * c + k, count, stride=48), :] = jnp.zeros((count, 128), f32)
    out_ref[...] = turned[...].astype(bf16).reshape(out_ref.shape)


def descend(core, hidden, other, down):
    count = hidden.shape[1] // CAP
    return pl.pallas_call(
        descend_kernel,
        in_specs=[pl.BlockSpec(memory_space=pltpu.SMEM)] + [whole] * 3,
        out_shape=jax.ShapeDtypeStruct((count, 48, 128), bf16),
        scratch_shapes=[pltpu.VMEM((4 * HD, CAP * count), bf16), pltpu.VMEM((count * 48, 128), f32)],
        compiler_params=pltpu.CompilerParams(vmem_limit_bytes=VM),
    )(core.reshape(1).astype(jnp.int32), hidden, other, down)


def combine_kernel(a_ref, x_ref, out_ref, scr):
    count = x_ref.shape[0]
    scr[...] = x_ref[...].astype(f32).reshape(scr.shape)
    for k in range(14):
        result = jnp.zeros((32, 128), f32)
        for c in range(CAP):
            result = result + dot(a_ref[c], scr[pl.ds(16 * c + k, count, stride=48), :].astype(bf16))
        out_ref[:, 128 * k : 128 * k + 128] = (result[:16] + result[16:]).astype(bf16)


def combine(weight, result):
    return pl.pallas_call(
        combine_kernel,
        out_shape=jax.ShapeDtypeStruct((16, DQ), bf16),
        scratch_shapes=[pltpu.VMEM((result.shape[0] * 48, 128), f32)],
        compiler_params=pltpu.CompilerParams(vmem_limit_bytes=VM),
    )(weight, result)


def per_device(store, queries, new_latent, cached_len, rows, expert_ids, route_gates, capacity):
    groups = lax.axis_size("sec")
    servers = groups // 4
    place = lax.axis_index("sec")
    part = lax.axis_index("tp")
    serving = place < servers
    both = ("sec", "tp")
    core = part % 2
    experts = capacity.shape[1]

    def across(value, d, first, last):
        return lax.ppermute(value, both, [(4 * q + t, 4 * q + (t ^ d)) for q in range(first, last) for t in range(4)])

    labels = jnp.arange(experts, dtype=jnp.int32)
    match = expert_ids[:, :, None] == labels[None, None, :]
    hits = jnp.any(match, axis=1).astype(jnp.int32)
    gate_of = jnp.sum(jnp.where(match, route_gates[:, :, None], 0.0), axis=1)
    rank = jnp.cumsum(hits, axis=0) - hits
    keep = (hits == 1) & (rank < capacity[0][None, :])
    slots = jnp.arange(CAP, dtype=jnp.int32)
    pick = (keep[None] & (rank[None] == slots[:, None, None])).astype(f32)

    def for_holders(value):
        return jnp.pad(jnp.repeat(value, 3, axis=2), ((0, 0), (0, 0), (servers, 0)))

    sel = jnp.swapaxes(for_holders(pick), 1, 2).astype(bf16)

    asked = ask(part, cached_len, jnp.swapaxes(queries, 1, 2))
    mine = [asked]
    for k in range(1, 4):
        mine.append(lax.ppermute(asked, "sec", [(k * servers + a, a) for a in range(servers)]))
    outgoing = dispatch(sel, rows)
    mine = stack(mine, outgoing[0, :16])
    (far,) = unpack(store, part, True, mine[0, :16])
    far = across(far, 2, servers, groups)

    def window():
        arrived = lax.all_to_all(outgoing, "sec", split_axis=0, concat_axis=0, tiled=True)
        other = across(mine, 1, 0, servers)
        here, down = unpack(store, part, False, outgoing[0, :16])
        parts = lax.cond(
            serving,
            lambda: tuple(attend(store, mine, other, part)),
            lambda: (jnp.zeros((256, PART), bf16),) * 4,
        )
        parts = [parts[0]] + [across(parts[d], d, 0, servers) for d in range(1, 4)]
        answer = lax.cond(serving, lambda: join(parts), lambda: jnp.zeros((256, PART), bf16))
        return arrived, here, down, answer

    def experts_part():
        slab = slots_of(arrived)
        beside = across(slab, 1, servers, groups)
        weights, _ = arrange(part, here, far, slab[:16, :128])
        partial = project(core, slab, weights)
        partial = project(1 - core, beside, weights, partial)
        partial = partial.astype(f32) + across(partial, 2, servers, groups).astype(f32)
        hidden = (jax.nn.silu(partial[: 2 * HD]) * partial[2 * HD :]).astype(bf16)
        return descend(core, hidden, across(hidden, 1, servers, groups), down)

    def way_back():
        back = lax.all_to_all(result, "sec", split_axis=0, concat_axis=0, tiled=True)
        shares = answer.reshape(4, 64, PART)
        returned = shares[0]
        for k in range(1, 4):
            returned = returned + lax.ppermute(shares[k], "sec", [(a, k * servers + a) for a in range(servers)])
        mine = lax.dynamic_slice_in_dim(queries, part * 32, 32, 1)
        own = jnp.einsum("rhk,rk->rh", mine, new_latent, preferred_element_type=f32) * softmax_scale
        own = own[:, :, None]
        returned = returned.reshape(2, 32, PART).astype(f32)
        others = returned[:, :, 512:513] + returned[:, :, 513:514] + returned[:, :, 514:515]
        top = jnp.maximum(own, others)
        own, others = jnp.exp(own - top), jnp.exp(others - top)
        attended = (others * returned[:, :, :LATENT] + own * new_latent[:, None, :LATENT].astype(f32)) / (own + others)

        scaled = for_holders(pick * gate_of[None])
        high = lax.reduce_precision(scaled, 8, 7)
        weight = jnp.concatenate([high, scaled - high], axis=1).astype(bf16)
        return combine(weight, back), attended.astype(bf16)

    def held(steps):
        shapes = jax.eval_shape(steps)
        return lax.cond(
            capacity[0, 0] >= 0, steps, lambda: jax.tree.map(lambda leaf: jnp.zeros(leaf.shape, leaf.dtype), shapes)
        )

    arrived, here, down, answer = held(window)
    result = held(experts_part)
    mixed, attended = held(way_back)

    return (attended, mixed)


def solution(mesh):
    placed = (
        P("sec", "tp", None),
        P("sec", None, None),
        P("sec", None),
        P("sec"),
        P("sec", "tp"),
        P("sec", None),
        P("sec", None),
        P("sec", None),
    )
    return jax.shard_map(
        per_device,
        mesh=mesh,
        in_specs=placed,
        out_specs=(P("sec", "tp", None), P("sec", "tp")),
        check_vma=False,
    )
```

```python
import functools
import math

import jax
import jax.numpy as jnp
from jax import lax
from jax.experimental import pallas as pl
from jax.experimental.pallas import tpu as pltpu
from jax.sharding import PartitionSpec as P

LATENT = 512
KV = 576
LP = 512
CAP = 3
HD = 96
DQ = 1792
PART = 640
f32 = jnp.float32
bf16 = jnp.bfloat16
VM = 16 << 20

softmax_scale = 1.0 / math.sqrt(192.0)


whole = pl.BlockSpec(memory_space=pltpu.VMEM)
after = pl.BlockSpec(memory_space=pl.ANY)


def dot(a, b, dims=((1,), (0,))):
    return lax.dot_general(a, b, (dims, ((), ())), preferred_element_type=f32)


def pieces(value):
    high = value.astype(bf16).astype(f32)
    middle = (value - high).astype(bf16).astype(f32)
    return high, middle, value - high - middle


def flat_rows(s_ref, scr):
    scr[...] = s_ref[...].astype(f32).reshape(scr.shape)


def dispatch_kernel(sel_ref, rows_ref, *refs):
    out_ref, scr = refs[-2:]
    source = lax.broadcasted_iota(jnp.int32, (256, 256), 0)
    target = lax.broadcasted_iota(jnp.int32, (256, 256), 1)
    order = (source == 4 * (target % 64) + target // 64).astype(f32).astype(bf16)
    count = out_ref.shape[0]
    for b in range(DQ // 256):
        turned = dot(rows_ref[:, 256 * b : 256 * b + 256], order).astype(bf16)
        for c in range(CAP):
            sent = dot(sel_ref[c], turned)
            for k in range(2):
                scr[pl.ds(16 * c + 2 * b + k, count, stride=48), :] = sent[:, 128 * k : 128 * k + 128]
    for c in range(CAP):
        for k in range(14, 16):
            scr[pl.ds(16 * c + k, count, stride=48), :] = jnp.zeros((count, 128), f32)
    out_ref[...] = scr[...].astype(bf16).reshape(out_ref.shape)


def dispatch(sel, rows, *earlier):
    groups = sel.shape[1]
    return pl.pallas_call(
        dispatch_kernel,
        in_specs=[whole] * 2 + [after] * len(earlier),
        out_shape=jax.ShapeDtypeStruct((groups, 48, 128), bf16),
        scratch_shapes=[pltpu.VMEM((groups * 48, 128), f32)],
        compiler_params=pltpu.CompilerParams(vmem_limit_bytes=VM),
    )(sel, rows, *earlier)


def ask_kernel(tp_ref, length_ref, q_ref, out_ref):
    out_ref[:KV] = q_ref[0]
    length = length_ref[tp_ref[0] % 2]
    row = lax.broadcasted_iota(jnp.int32, (16, 128), 0)
    out_ref[KV:] = jnp.where(row == 0, length // 64, length % 64).astype(f32).astype(bf16)


def ask(part, lengths, queries):
    return pl.pallas_call(
        ask_kernel,
        grid_spec=pltpu.PrefetchScalarGridSpec(
            num_scalar_prefetch=2,
            grid=(1,),
            in_specs=[pl.BlockSpec((1, KV, 128), lambda i, tp, lengths: (tp[0] % 2, 0, 0))],
            out_specs=pl.BlockSpec((KV + 16, 128), lambda i, tp, lengths: (0, 0)),
        ),
        out_shape=jax.ShapeDtypeStruct((KV + 16, 128), bf16),
    )(part.reshape(1).astype(jnp.int32), lengths, queries)


def stack_kernel(*refs):
    for n in range(4):
        refs[-1][n] = refs[n][...]


def stack(rows, earlier):
    return pl.pallas_call(
        stack_kernel,
        in_specs=[whole] * 4 + [after],
        out_shape=jax.ShapeDtypeStruct((4,) + rows[0].shape, bf16),
    )(*rows, earlier)


def attend_kernel(tp_ref, s_ref, mine_ref, other_ref, *refs):
    p_refs, (scr, keys, found) = refs[:4], refs[4:]
    step = pl.program_id(0)
    row = served(step, tp_ref)
    flat_rows(s_ref, scr)
    for m in range(9):
        keys[:, 128 * m : 128 * m + 128] = scr[pl.ds(m, LP // 2, stride=9), :].astype(bf16)
    asked = jnp.where(step < 4, mine_ref[0].astype(f32), other_ref[0].astype(f32))
    left = asked[KV : KV + 1, 0:1] * 64.0 + asked[KV + 1 : KV + 2, 0:1] - (tp_ref[0] * LP).astype(f32)
    gap = jnp.zeros((64, 128), f32)
    even_q = jnp.concatenate([asked[:KV], gap], axis=0).T.astype(bf16)
    odd_q = jnp.concatenate([gap, asked[:KV]], axis=0).T.astype(bf16)
    even = dot(even_q, keys[:, :640], ((1,), (1,))) * softmax_scale
    odd = dot(odd_q, keys[:, 512:], ((1,), (1,))) * softmax_scale
    position = (2 * lax.broadcasted_iota(jnp.int32, (128, LP // 2), 1)).astype(f32)
    even = jnp.where(position < left, even, -1e30)
    odd = jnp.where(position + 1.0 < left, odd, -1e30)
    top = jnp.maximum(jnp.max(even, axis=1, keepdims=True), jnp.max(odd, axis=1, keepdims=True))
    even = jnp.where(position < left, jnp.exp(even - top), 0.0).astype(bf16)
    odd = jnp.where(position + 1.0 < left, jnp.exp(odd - top), 0.0).astype(bf16)
    total = jnp.sum(even.astype(f32), axis=1, keepdims=True) + jnp.sum(odd.astype(f32), axis=1, keepdims=True)
    summed = dot(even, keys[:, :LATENT]) + dot(odd, keys[:, 512:])[:, 64 : 64 + LATENT]
    lane = lax.broadcasted_iota(jnp.int32, (128, 128), 1)
    stats = jnp.zeros((128, 128), f32)
    for at, piece in enumerate(pieces(top) + pieces(total)):
        stats = jnp.where(lane == at, piece, stats)
    found[:, :LATENT] = summed.astype(bf16)
    found[:, LATENT:] = stats.astype(bf16)
    span = pl.ds(pl.multiple_of(row * 32, 32), 32)
    for d, p_ref in enumerate(p_refs):
        share = pl.multiple_of(jnp.bitwise_xor(tp_ref[0], d) * 32, 32)
        p_ref[span, :] = found[pl.ds(share, 32), :]


def served(step, tp):
    return 2 * (step % 4) + jnp.bitwise_xor(tp[0] % 2, step // 4)


def attend(store, mine, other, part):
    shape = (256, PART)
    rows = (1,) + mine.shape[1:]
    return pl.pallas_call(
        attend_kernel,
        grid_spec=pltpu.PrefetchScalarGridSpec(
            num_scalar_prefetch=1,
            grid=(8,),
            in_specs=[
                pl.BlockSpec((1, 1, LP * KV), lambda i, tp: (0, 0, served(i, tp))),
                pl.BlockSpec(rows, lambda i, tp: (jnp.minimum(i, 3), 0, 0)),
                pl.BlockSpec(rows, lambda i, tp: (jnp.maximum(i - 4, 0), 0, 0)),
            ],
            out_specs=[pl.BlockSpec(shape, lambda i, tp: (0, 0))] * 4,
            scratch_shapes=[
                pltpu.VMEM((LP * KV // 128, 128), f32),
                pltpu.VMEM((LP // 2, 2 * KV), bf16),
                pltpu.VMEM((128, PART), bf16),
            ],
        ),
        out_shape=[jax.ShapeDtypeStruct(shape, bf16)] * 4,
        compiler_params=pltpu.CompilerParams(vmem_limit_bytes=VM),
    )(part.reshape(1).astype(jnp.int32), store, mine, other)


def unpack_kernel(tp_ref, s_ref, _, p_ref, *refs):
    scr = refs[-1]
    step = pl.program_id(0)
    flat_rows(s_ref, scr)

    @pl.when(step < 4)
    def _():
        for m in range(3):
            p_ref[:, 128 * m : 128 * m + 128] = scr[pl.ds(m, 448, stride=3), :].astype(bf16)

    if len(refs) > 1:
        w_ref = refs[0]

        @pl.when(step >= 4)
        def _():
            for m in range(14):
                w_ref[:, 128 * m : 128 * m + 128] = scr[pl.ds(m, HD, stride=14), :].astype(bf16)


def unpack(store, part, far, earlier):
    def block(i, tp):
        x_hi = jnp.bitwise_xor(tp[0] // 2, 1 if far else 0)
        return 0, 0, jnp.where(i < 4, 4 * (i // 2) + 2 * x_hi + i % 2, i + 4)

    out_specs = [pl.BlockSpec((448, 384), lambda i, tp: (jnp.minimum(i, 3), 0))]
    out_shape = [jax.ShapeDtypeStruct((DQ, 384), bf16)]
    if not far:
        out_specs.append(pl.BlockSpec((HD, DQ), lambda i, tp: (jnp.maximum(i - 4, 0), 0)))
        out_shape.append(jax.ShapeDtypeStruct((4 * HD, DQ), bf16))
    return pl.pallas_call(
        unpack_kernel,
        grid_spec=pltpu.PrefetchScalarGridSpec(
            num_scalar_prefetch=1,
            grid=(4 if far else 8,),
            in_specs=[pl.BlockSpec((1, 1, DQ * HD), block), after],
            out_specs=out_specs,
            scratch_shapes=[pltpu.VMEM((DQ * HD // 128, 128), f32)],
        ),
        out_shape=out_shape,
        compiler_params=pltpu.CompilerParams(vmem_limit_bytes=VM),
    )(part.reshape(1).astype(jnp.int32), store, earlier)


def weights_kernel(tp_ref, here_ref, far_ref, _, w_ref, mark_ref):
    mark_ref[...] = jnp.zeros_like(mark_ref)

    def fill(refs):
        for half in range(2):
            for q in range(2):
                rows = slice(896 * half + 448 * q, 896 * half + 448 * q + 448)
                for r in range(4):
                    found = jnp.concatenate([ref[rows, HD * r : HD * r + HD] for ref in refs], axis=1)
                    for b in range(7):
                        at = DQ * q + 256 * b + 64 * r
                        w_ref[half, at : at + 64, :] = found[64 * b : 64 * b + 64]

    @pl.when(tp_ref[0] < 2)
    def _():
        fill((here_ref, far_ref))

    @pl.when(tp_ref[0] >= 2)
    def _():
        fill((far_ref, here_ref))


def arrange(part, here, far, earlier):
    return pl.pallas_call(
        weights_kernel,
        in_specs=[pl.BlockSpec(memory_space=pltpu.SMEM), whole, whole, after],
        out_shape=[jax.ShapeDtypeStruct((2, 2 * DQ, 2 * HD), bf16), jax.ShapeDtypeStruct((8, 128), f32)],
        compiler_params=pltpu.CompilerParams(vmem_limit_bytes=VM),
    )(part.reshape(1).astype(jnp.int32), here, far, earlier)


def join_kernel(p0_ref, p1_ref, p2_ref, p3_ref, out_ref):
    refs = (p0_ref, p1_ref, p2_ref, p3_ref)
    tops, totals = [], []
    for p_ref in refs:
        stats = p_ref[:, LATENT:].astype(f32)
        tops.append(stats[:, 0:1] + stats[:, 1:2] + stats[:, 2:3])
        totals.append(stats[:, 3:4] + stats[:, 4:5] + stats[:, 5:6])
    top = functools.reduce(jnp.maximum, tops)
    scales = [jnp.exp(own - top) for own in tops]
    total = sum(scale * own for scale, own in zip(scales, totals))
    scales = [scale / total for scale in scales]
    out_ref[:, :LATENT] = sum(
        scale * p_ref[:, :LATENT].astype(f32) for scale, p_ref in zip(scales, refs)
    ).astype(bf16)
    lane = lax.broadcasted_iota(jnp.int32, (256, 128), 1)
    stats = jnp.zeros((256, 128), f32)
    for at, piece in enumerate(pieces(top + jnp.log(total))):
        stats = jnp.where(lane == at, piece, stats)
    out_ref[:, LATENT:] = stats.astype(bf16)


def join(parts):
    return pl.pallas_call(
        join_kernel,
        out_shape=jax.ShapeDtypeStruct((256, PART), bf16),
        compiler_params=pltpu.CompilerParams(vmem_limit_bytes=VM),
    )(*parts)


def slab_kernel(x_ref, *refs):
    out_ref, scr = refs[-2:]
    count = x_ref.shape[0]
    scr[...] = x_ref[...].astype(f32).reshape(scr.shape)
    for c in range(CAP):
        for k in range(14):
            found = scr[pl.ds(16 * c + k, count, stride=48), :].astype(bf16)
            out_ref[count * c : count * c + count, 128 * k : 128 * k + 128] = found


def slots_of(arrived, *earlier):
    count = arrived.shape[0]
    return pl.pallas_call(
        slab_kernel,
        in_specs=[whole] + [after] * len(earlier),
        out_shape=jax.ShapeDtypeStruct((CAP * count, DQ), bf16),
        scratch_shapes=[pltpu.VMEM((count * 48, 128), f32)],
        compiler_params=pltpu.CompilerParams(vmem_limit_bytes=VM),
    )(arrived, *earlier)


def project_kernel(_, x_ref, w_ref, *refs):
    z_ref = refs[-1]
    for half in range(2):
        found = dot(x_ref[...], w_ref[half])
        if len(refs) > 1:
            found = found + refs[0][half]
            z_ref[2 * HD * half : 2 * HD * half + 2 * HD, :] = found.T.astype(bf16)
        else:
            z_ref[half] = found


def project(core, slab, weights, *other):
    slots = slab.shape[0]
    if other:
        shape = jax.ShapeDtypeStruct((4 * HD, slots), bf16)
    else:
        shape = jax.ShapeDtypeStruct((2, slots, 2 * HD), f32)
    full = lambda array: pl.BlockSpec(array.shape, lambda i, core: (0,) * len(array.shape))
    return pl.pallas_call(
        project_kernel,
        grid_spec=pltpu.PrefetchScalarGridSpec(
            num_scalar_prefetch=1,
            grid=(1,),
            in_specs=[full(slab), pl.BlockSpec((2, DQ, 2 * HD), lambda i, core: (0, core[0], 0))]
            + [full(sums) for sums in other],
            out_specs=full(shape),
        ),
        out_shape=shape,
        compiler_params=pltpu.CompilerParams(vmem_limit_bytes=VM),
    )(core.reshape(1).astype(jnp.int32), slab, weights, *other)


def descend_kernel(core_ref, h_ref, o_ref, w_ref, out_ref, scr, turned):
    count = out_ref.shape[0]
    core = core_ref[0]
    for x_hi in range(2):
        rows = slice(HD * x_hi, HD * x_hi + HD)
        for at, ref in ((2 * x_hi + core, h_ref), (2 * x_hi + 1 - core, o_ref)):
            scr[pl.ds(pl.multiple_of(at * HD, HD), HD), :] = ref[rows]
    for c in range(CAP):
        result = dot(scr[:, count * c : count * c + count], w_ref[...], ((0,), (0,)))
        for k in range(14):
            turned[pl.ds(16 * c + k, count, stride=48), :] = result[:, 128 * k : 128 * k + 128]
        for k in range(14, 16):
            turned[pl.ds(16 * c + k, count, stride=48), :] = jnp.zeros((count, 128), f32)
    out_ref[...] = turned[...].astype(bf16).reshape(out_ref.shape)


def descend(core, hidden, other, down):
    count = hidden.shape[1] // CAP
    return pl.pallas_call(
        descend_kernel,
        in_specs=[pl.BlockSpec(memory_space=pltpu.SMEM)] + [whole] * 3,
        out_shape=jax.ShapeDtypeStruct((count, 48, 128), bf16),
        scratch_shapes=[pltpu.VMEM((4 * HD, CAP * count), bf16), pltpu.VMEM((count * 48, 128), f32)],
        compiler_params=pltpu.CompilerParams(vmem_limit_bytes=VM),
    )(core.reshape(1).astype(jnp.int32), hidden, other, down)


def combine_kernel(a_ref, x_ref, out_ref, scr):
    count = x_ref.shape[0]
    scr[...] = x_ref[...].astype(f32).reshape(scr.shape)
    for k in range(14):
        result = jnp.zeros((32, 128), f32)
        for c in range(CAP):
            result = result + dot(a_ref[c], scr[pl.ds(16 * c + k, count, stride=48), :].astype(bf16))
        out_ref[:, 128 * k : 128 * k + 128] = (result[:16] + result[16:]).astype(bf16)


def combine(weight, result):
    return pl.pallas_call(
        combine_kernel,
        out_shape=jax.ShapeDtypeStruct((16, DQ), bf16),
        scratch_shapes=[pltpu.VMEM((result.shape[0] * 48, 128), f32)],
        compiler_params=pltpu.CompilerParams(vmem_limit_bytes=VM),
    )(weight, result)


def per_device(store, queries, new_latent, cached_len, rows, expert_ids, route_gates, capacity):
    groups = lax.axis_size("sec")
    servers = groups // 4
    place = lax.axis_index("sec")
    part = lax.axis_index("tp")
    serving = place < servers
    both = ("sec", "tp")
    core = part % 2
    experts = capacity.shape[1]

    def across(value, d, first, last):
        return lax.ppermute(value, both, [(4 * q + t, 4 * q + (t ^ d)) for q in range(first, last) for t in range(4)])

    labels = jnp.arange(experts, dtype=jnp.int32)
    match = expert_ids[:, :, None] == labels[None, None, :]
    hits = jnp.any(match, axis=1).astype(jnp.int32)
    gate_of = jnp.sum(jnp.where(match, route_gates[:, :, None], 0.0), axis=1)
    rank = jnp.cumsum(hits, axis=0) - hits
    keep = (hits == 1) & (rank < capacity[0][None, :])
    slots = jnp.arange(CAP, dtype=jnp.int32)
    pick = (keep[None] & (rank[None] == slots[:, None, None])).astype(f32)

    def for_holders(value):
        return jnp.pad(jnp.repeat(value, 3, axis=2), ((0, 0), (0, 0), (servers, 0)))

    sel = jnp.swapaxes(for_holders(pick), 1, 2).astype(bf16)

    asked = ask(part, cached_len, jnp.swapaxes(queries, 1, 2))
    mine = [asked]
    for k in range(1, 4):
        mine.append(lax.ppermute(asked, "sec", [(k * servers + a, a) for a in range(servers)]))
    outgoing = dispatch(sel, rows)
    received = jnp.concatenate([row[:16] for row in mine[1:]] + [outgoing[0, :16]], axis=0)
    (far,) = unpack(store, part, True, received)
    far = across(far, 2, servers, groups)

    def window():
        arrived = lax.all_to_all(outgoing, "sec", split_axis=0, concat_axis=0, tiled=True)
        rows_here = stack(mine, received)
        other = across(rows_here, 1, 0, servers)
        here, down = unpack(store, part, False, outgoing[0, :16])
        parts = lax.cond(
            serving,
            lambda: tuple(attend(store, rows_here, other, part)),
            lambda: (jnp.zeros((256, PART), bf16),) * 4,
        )
        parts = [parts[0]] + [across(parts[d], d, 0, servers) for d in range(1, 4)]
        answer = lax.cond(serving, lambda: join(parts), lambda: jnp.zeros((256, PART), bf16))
        return arrived, here, down, answer

    def experts_part():
        slab = slots_of(arrived)
        beside = across(slab, 1, servers, groups)
        weights, _ = arrange(part, here, far, slab[:16, :128])
        partial = project(core, slab, weights)
        partial = project(1 - core, beside, weights, partial)
        partial = partial.astype(f32) + across(partial, 2, servers, groups).astype(f32)
        hidden = (jax.nn.silu(partial[: 2 * HD]) * partial[2 * HD :]).astype(bf16)
        return descend(core, hidden, across(hidden, 1, servers, groups), down)

    def way_back():
        back = lax.all_to_all(result, "sec", split_axis=0, concat_axis=0, tiled=True)
        shares = answer.reshape(4, 64, PART)
        returned = shares[0]
        for k in range(1, 4):
            returned = returned + lax.ppermute(shares[k], "sec", [(a, k * servers + a) for a in range(servers)])
        mine = lax.dynamic_slice_in_dim(queries, part * 32, 32, 1)
        own = jnp.einsum("rhk,rk->rh", mine, new_latent, preferred_element_type=f32) * softmax_scale
        own = own[:, :, None]
        returned = returned.reshape(2, 32, PART).astype(f32)
        others = returned[:, :, 512:513] + returned[:, :, 513:514] + returned[:, :, 514:515]
        top = jnp.maximum(own, others)
        own, others = jnp.exp(own - top), jnp.exp(others - top)
        attended = (others * returned[:, :, :LATENT] + own * new_latent[:, None, :LATENT].astype(f32)) / (own + others)

        scaled = for_holders(pick * gate_of[None])
        high = lax.reduce_precision(scaled, 8, 7)
        weight = jnp.concatenate([high, scaled - high], axis=1).astype(bf16)
        return combine(weight, back), attended.astype(bf16)

    def held(steps):
        shapes = jax.eval_shape(steps)
        return lax.cond(
            capacity[0, 0] >= 0, steps, lambda: jax.tree.map(lambda leaf: jnp.zeros(leaf.shape, leaf.dtype), shapes)
        )

    arrived, here, down, answer = held(window)
    result = held(experts_part)
    mixed, attended = held(way_back)

    return (attended, mixed)


def solution(mesh):
    placed = (
        P("sec", "tp", None),
        P("sec", None, None),
        P("sec", None),
        P("sec"),
        P("sec", "tp"),
        P("sec", None),
        P("sec", None),
        P("sec", None),
    )
    return jax.shard_map(
        per_device,
        mesh=mesh,
        in_specs=placed,
        out_specs=(P("sec", "tp", None), P("sec", "tp")),
        check_vma=False,
    )
```
